128 devices in a mesh: slide: 8 (over x, core), enc: 16 (over y, z).
Axes of the slice: x: 4, y: 4, z: 4, core: 2. Of those that a mesh axis runs over, the one named last changes fastest.
Arguments:
- tile_maps: bfloat16 [8, 512, 7, 7, 768], P('slide', 'enc'), may hold values from -6 to 6
- tile_owner: int32 [8, 512, 1], P('slide', 'enc'), may hold values from 0 to 15; in each aligned block of 32 rows (0 to 31, 32 to 63, ..., all dimensions but the last counted through in order) at most 3 rows name the same one
- tissue_counts: int32 [8, 16], P('slide'), may hold values from 1 to 32, as said below
- embed_grad: bfloat16 [8, 16, 16, 3, 768], P('slide', 'enc'), may hold values from -1.5 to 1.5
- depth_kernel: bfloat16 [7, 7, 768], replicated, may hold values from -0.875 to 0.875
- up_weight: bfloat16 [3072, 768], replicated, may hold values from -0.21875 to 0.21875
- down_weight: bfloat16 [3072, 768], replicated, may hold values from -0.109375 to 0.109375
Outputs:
- slide_embed: bfloat16 [8, 16, 16, 3, 768], P('slide', 'enc')
- up_grad: float32 [3072, 768], P(('slide', 'enc'))
- down_grad: float32 [3072, 768], P(('slide', 'enc'))
The draws below stay inside these ranges and needn't reach their ends.
Inputs may be any that keep to these rules, and one draw needn't show every extreme that they name: `tissue_counts`: within one slide row, a reader's count plus the count of the reader half the enc axis away is at most 48; some pair reaches it. `tile_owner`: among the 32 slots of one reader no owner is named more than 3 times; some reader reaches it.
All inputs are finite; a program needn't handle non-finite values.
Results may differ from the reference program's by a relative error of at most 0.015.
Values may be sent and summed in bfloat16 or wider, within the bound.
No kernel may reach another device: no remote copies, remote signals or barrier semaphores. Data moves between devices by JAX's collectives and lax.ppermute only.
A program may use at most 256 MiB of HBM per device.

```python
import math
import jax
import jax.numpy as jnp
import numpy as np
from jax import lax

D = 768
FF = 3072
SIDE = 7
TILES_DEV = 32
WORK = 24
PAIR_CAP = 3
N_SLIDE = 8
N_ENC = 16


def draw_tissue_counts(key, part):
    key = jax.random.fold_in(key, 11)
    halfway = N_ENC // 2
    key_total, key_split, key_pick = jax.random.split(key, 3)
    totals = jax.random.randint(key_total, (N_SLIDE, halfway), TILES_DEV, 2 * WORK + 1, dtype=jnp.int32)
    chosen = jax.random.randint(key_pick, (), 0, N_SLIDE * halfway, dtype=jnp.int32)
    flat_index = jnp.arange(N_SLIDE * halfway, dtype=jnp.int32).reshape(N_SLIDE, halfway)
    totals = jnp.where(flat_index == chosen, 2 * WORK, totals)
    lower_end = jnp.maximum(1, totals - TILES_DEV)
    upper_end = jnp.minimum(TILES_DEV, totals - 1)
    first_part = jax.random.randint(key_split, (N_SLIDE, halfway), lower_end, upper_end + 1, dtype=jnp.int32)
    second_part = totals - first_part
    return jnp.concatenate([first_part, second_part], axis=1).astype(jnp.int32)


def levels(own_key, shape, shards, smallest, largest):
    def one(dim, blocks):
        steps = jax.random.uniform(jax.random.fold_in(jax.random.fold_in(own_key, 6), dim), (blocks,), jnp.float32, smallest / len(shards), largest / len(shards))
        return jnp.repeat(jnp.exp(steps), shape[dim] // blocks).reshape((-1,) + (1,) * (len(shape) - dim - 1))

    gain = one(*shards[0])
    for cut in shards[1:]:
        gain = gain * one(*cut)
    return gain


def shared_out(rng, own, number, rows, amount, top, most, skew):
    order = jax.random.permutation(rng, amount)
    packed, usual = portions_of(amount, rows * top, most, skew, True), portions_of(amount, rows * top, most, skew, False)
    places = jnp.arange(amount)

    def named(sizes, rotation):
        used = int((sizes > 0).sum())
        fixed = max(1, used // 4)
        shifted = fixed + (places - fixed + rotation * (used - fixed)) % max(1, amount - fixed)
        return jnp.zeros((amount,), jnp.int32).at[order[jnp.where(places < fixed, places, shifted)]].set(jnp.asarray(sizes, jnp.int32))

    sizes = jnp.where(number % 4 == 0, named(packed, number // 4), named(usual, number - number // 4 - 1))
    mixed = jax.random.permutation(jax.random.fold_in(own, 3), amount)
    giver, receiver = mixed[0:amount // 2 * 2:2], mixed[1:amount // 2 * 2:2]
    room = jnp.minimum(sizes[giver] - 1, most - sizes[receiver]) // 2
    room = jnp.where((giver == order[0]) | (receiver == order[0]) | (sizes[receiver] == 0), 0, jnp.maximum(room, 0))
    shifted = jax.random.randint(jax.random.fold_in(own, 4), (amount // 2,), 0, 1 << 20) % (room + 1)
    sizes = sizes.at[giver].add(-shifted).at[receiver].add(shifted)
    labels = jnp.searchsorted(jnp.cumsum(sizes), jnp.arange(rows * top), side="right").astype(jnp.int32)
    grid = labels.reshape(top, rows).T
    grid = grid[jax.random.permutation(jax.random.fold_in(own, 1), rows)]
    rotation = jax.random.randint(jax.random.fold_in(own, 2), (rows, 1), 0, top)
    return jnp.take_along_axis(grid, (jnp.arange(top)[None, :] + rotation) % top, axis=1)


def portions_of(amount, total, bound, slope, full):
    loads = [(1 << 20) // math.isqrt(rank ** slope) + 1 for rank in range(1, amount + 1)]
    largest = bound if full else min(bound, max(-(-total // amount), total * loads[0] // sum(loads)))
    least = 1 if total - largest >= amount - 1 else 0
    given, rest = [largest] + [least] * (amount - 1), total - largest - least * (amount - 1)
    while rest > 0:
        free = [i for i in range(1, amount) if given[i] < largest] or [i for i in range(1, amount) if given[i] < bound]
        whole, remaining = sum([loads[i] for i in free]), rest
        for i in free:
            extra = min(bound - given[i], max(1, remaining * loads[i] // whole), rest)
            given[i] = given[i] + extra
            rest = rest - extra
    return np.array(given)


def gaussian(own_key, dims, deviation, bound, cuts=(), kind=jnp.bfloat16):
    gain = levels(own_key, dims, cuts, -0.22, 0.18) if cuts else 1.0
    array = jax.random.normal(own_key, dims, jnp.float32) * deviation * gain
    return jnp.minimum(jnp.maximum(array, -bound), bound).astype(kind)


def setup_inputs(seed: int = 0) -> dict:
    key_list = jax.random.split(jax.random.key(seed), 8)
    tile_maps = gaussian(key_list[0], (N_SLIDE, N_ENC * TILES_DEV, SIDE, SIDE, D), 1.0, 6.0, ((0, 8), (1, 16)))
    tile_owner_keys = jax.random.split(jax.random.fold_in(key_list[1], 1), N_SLIDE * (N_ENC * TILES_DEV) // TILES_DEV)
    tile_owner_turns = jax.random.permutation(jax.random.fold_in(key_list[1], 3), N_SLIDE * (N_ENC * TILES_DEV) // TILES_DEV)
    tile_owner = jax.vmap(lambda own, number: shared_out(jax.random.fold_in(key_list[1], 2), own, number, TILES_DEV, N_ENC, 1, PAIR_CAP, 2))(tile_owner_keys, tile_owner_turns).reshape((N_SLIDE, N_ENC * TILES_DEV, 1))
    tissue_counts = draw_tissue_counts(jax.random.fold_in(key_list[7], 71), 0)
    embed_grad = gaussian(key_list[3], (N_SLIDE, N_ENC, N_ENC, PAIR_CAP, D), 0.25, 1.5, ((0, 8), (1, 16)))
    depth_kernel = gaussian(key_list[4], (SIDE, SIDE, D), (SIDE * SIDE) ** -0.5, 0.875)
    up_weight = gaussian(key_list[5], (FF, D), D ** -0.5, 0.21875)
    down_weight = gaussian(key_list[6], (FF, D), FF ** -0.5, 0.109375)
    return dict(tile_maps=tile_maps, tile_owner=tile_owner, tissue_counts=tissue_counts, embed_grad=embed_grad, depth_kernel=depth_kernel, up_weight=up_weight, down_weight=down_weight)


root_half = 0.7071067811865476
inv_root_two_pi = 0.3989422804014327

def depthwise(feature_maps, kernel):
    map_side = feature_maps.shape[1]
    kernel_reach = kernel.shape[0] // 2
    padded = jnp.pad(feature_maps, ((0, 0), (kernel_reach, kernel_reach), (kernel_reach, kernel_reach), (0, 0)))
    result = jnp.zeros(feature_maps.shape, jnp.float32)
    for row_shift in range(kernel.shape[0]):
        for col_shift in range(kernel.shape[1]):
            window = padded[:, row_shift:row_shift + map_side, col_shift:col_shift + map_side, :]
            result = result + window.astype(jnp.float32) * kernel[row_shift, col_shift].astype(jnp.float32)
    return result

def gelu_slope(values):
    return 0.5 * (1.0 + jax.scipy.special.erf(values * root_half)) + values * jnp.exp(-0.5 * values * values) * inv_root_two_pi

def tile_pass(feature_maps, slot_grad, depth_kernel, up_weight, down_weight):
    tile_total = feature_maps.shape[0]
    cell_total = feature_maps.shape[1] * feature_maps.shape[2]
    feature_width = feature_maps.shape[3]
    conv = depthwise(feature_maps, depth_kernel)
    channel_mean = lax.optimization_barrier(jnp.mean(conv, axis=-1, keepdims=True))
    centred = conv - channel_mean
    channel_var = lax.optimization_barrier(jnp.mean(centred * centred, axis=-1, keepdims=True))
    normed = (centred * lax.rsqrt(channel_var + 1e-06)).astype(jnp.bfloat16).reshape(tile_total * cell_total, feature_width)
    pre = lax.dot_general(normed, up_weight, (((1,), (1,)), ((), ())), preferred_element_type=jnp.float32)
    hidden = jax.nn.gelu(pre, approximate=False).astype(jnp.bfloat16)
    mixed = jnp.dot(hidden, down_weight, preferred_element_type=jnp.float32)
    block_out = feature_maps.reshape(tile_total * cell_total, feature_width).astype(jnp.float32) + mixed
    tile_embed = lax.optimization_barrier(jnp.mean(block_out.reshape(tile_total, cell_total, feature_width), axis=1)).astype(jnp.bfloat16)
    dhidden = lax.dot_general(slot_grad, down_weight, (((1,), (1,)), ((), ())), preferred_element_type=jnp.float32) / cell_total
    slope_value = gelu_slope(pre).reshape(tile_total, cell_total, -1)
    pre_grad = (slope_value * dhidden[:, None, :]).reshape(tile_total * cell_total, -1).astype(jnp.bfloat16)
    pooled = lax.optimization_barrier(jnp.mean(hidden.reshape(tile_total, cell_total, -1).astype(jnp.float32), axis=1)).astype(jnp.bfloat16)
    return (tile_embed, normed, pre_grad, pooled)

def slot_table(owners, own_count, owner_total, capacity):
    slot_total = owners.shape[0]
    live = jnp.arange(slot_total, dtype=jnp.int32) < own_count
    match = ((owners[:, None] == jnp.arange(owner_total, dtype=jnp.int32)[None, :]) & live[:, None]).astype(jnp.int32)
    earlier = jnp.cumsum(match, axis=0, dtype=jnp.int32) - match
    rank = lax.optimization_barrier(jnp.sum(earlier * match, axis=1, dtype=jnp.int32))
    target = owners * capacity + rank
    chosen = (target[:, None] == jnp.arange(owner_total * capacity, dtype=jnp.int32)[None, :]) & live[:, None]
    return chosen.astype(jnp.bfloat16)

def reference(tile_maps, tile_owner, tissue_counts, embed_grad, depth_kernel, up_weight, down_weight):
    reader_total = N_SLIDE * N_ENC
    all_maps = tile_maps.reshape(reader_total, TILES_DEV, SIDE, SIDE, D)
    all_owners = tile_owner.reshape(reader_total, TILES_DEV)
    all_counts = tissue_counts.reshape(reader_total)
    all_grads = jnp.transpose(embed_grad, (0, 2, 1, 3, 4)).reshape(reader_total, N_ENC * PAIR_CAP, D)

    def reader_step(running, inputs):
        block_maps, owners, own_count, owner_grads = inputs
        select_table = slot_table(owners, own_count, N_ENC, PAIR_CAP)
        slot_grad = jnp.dot(select_table, owner_grads, preferred_element_type=jnp.float32).astype(jnp.bfloat16)
        tile_embed, normed, pre_grad, pooled = tile_pass(block_maps, slot_grad, depth_kernel, up_weight, down_weight)
        up_term = lax.dot_general(pre_grad, normed, (((0,), (0,)), ((), ())), preferred_element_type=jnp.float32)
        down_term = lax.dot_general(pooled, slot_grad, (((0,), (0,)), ((), ())), preferred_element_type=jnp.float32)
        sent = lax.dot_general(select_table, tile_embed, (((0,), (0,)), ((), ())), preferred_element_type=jnp.float32).astype(jnp.bfloat16)
        return ((running[0] + up_term, running[1] + down_term), sent)
    start_value = (jnp.zeros((FF, D), jnp.float32), jnp.zeros((FF, D), jnp.float32))
    summed, sends = lax.scan(reader_step, start_value, (all_maps, all_owners, all_counts, all_grads))
    slide_embed = jnp.transpose(sends.reshape(N_SLIDE, N_ENC, N_ENC, PAIR_CAP, D), (0, 2, 1, 3, 4))
    return (slide_embed, summed[0], summed[1])
```

```python
import functools

import jax
import jax.numpy as jnp
from jax import lax
from jax.experimental import pallas as pl
from jax.experimental.pallas import tpu as pltpu
from jax.sharding import PartitionSpec as P

root_half = 0.7071067811865476
inv_root_two_pi = 0.3989422804014327
axes = ("slide", "enc")
hops = (2, 1, 3)
VMEM = pl.BlockSpec(memory_space=pltpu.VMEM)
nt = (((1,), (1,)), ((), ()))
tn = (((0,), (0,)), ((), ()))


def f32_dot(lhs, rhs, dims=(((1,), (0,)), ((), ()))):
    return lax.dot_general(lhs, rhs, dims, preferred_element_type=jnp.float32)


def conv_kernel(x_ref, k_ref, normed_ref, mean_ref, xf, kf, cv):
    side = x_ref.shape[0]
    tiles, width = x_ref.shape[2:]
    cells = side * side
    for n in range(cells):
        kf[n] = jnp.broadcast_to(
            k_ref[n // side, n % side : n % side + 1].astype(jnp.float32), (8, width)
        )

    @pl.loop(0, tiles // 16)
    def _(group):
        row = pl.multiple_of(group * 16, 16)
        for n in range(cells):
            xf[n] = x_ref[n // side, n % side, pl.ds(row, 16), :].astype(jnp.float32)

        @pl.loop(0, 2 * (width // 128))
        def _(unit):
            lane = pl.multiple_of((unit // 2) * 128, 128)
            half = pl.multiple_of((unit % 2) * 8, 8)
            for i in range(side):
                acc = [None] * side
                for a in range(side):
                    r = i + a - side // 2
                    if not 0 <= r < side:
                        continue
                    xs = [xf[r * side + j, pl.ds(half, 8), pl.ds(lane, 128)] for j in range(side)]
                    ks = [kf[a * side + b, :, pl.ds(lane, 128)] for b in range(side)]
                    for j in range(side):
                        for b in range(side):
                            c = j + b - side // 2
                            if 0 <= c < side:
                                term = xs[c] * ks[b]
                                acc[j] = term if acc[j] is None else acc[j] + term
                for j in range(side):
                    cv[i * side + j, pl.ds(half, 8), pl.ds(lane, 128)] = acc[j]

        total = None
        for n in range(cells):
            conv = cv[n]
            centred = conv - jnp.sum(conv, axis=1, keepdims=True) * (1.0 / width)
            var = jnp.sum(centred * centred, axis=1, keepdims=True) * (1.0 / width)
            normed_ref[n, pl.ds(row, 16), :] = (centred * lax.rsqrt(var + 1e-6)).astype(jnp.bfloat16)
            total = xf[n] if total is None else total + xf[n]
        mean_ref[pl.ds(row, 16), :] = total * (1.0 / cells)


def conv_norm(maps, kernel):
    side, _, tiles, width = maps.shape
    cells = side * side
    return pl.pallas_call(
        conv_kernel,
        out_shape=(
            jax.ShapeDtypeStruct((cells, tiles, width), jnp.bfloat16),
            jax.ShapeDtypeStruct((tiles, width), jnp.float32),
        ),
        in_specs=[VMEM] * 2,
        out_specs=(VMEM, VMEM),
        scratch_shapes=[
            pltpu.VMEM((cells, 16, width), jnp.float32),
            pltpu.VMEM((cells, 8, width), jnp.float32),
            pltpu.VMEM((cells, 16, width), jnp.float32),
        ],
        compiler_params=pltpu.CompilerParams(vmem_limit_bytes=24 << 20),
        cost_estimate=pl.CostEstimate(
            flops=15_000_000_000, bytes_accessed=5_000_000, transcendentals=0
        ),
        name="conv_norm",
    )(maps, kernel)


def gelu_pair(pre):
    cdf = 0.5 + 0.5 * lax.erf(pre * root_half)
    density = jnp.exp(pre * pre * -0.5) * inv_root_two_pi
    return pre * cdf, cdf + pre * density


def block_kernel(
    starts, own_ref, sib_ref, sgo_ref, sgs_ref, *rest
):
    ups, downs = rest[0:4], rest[4:8]
    emb_ref, pay_ref, emb_out, up_s, dn_s, bo, bs = rest[8:]
    units = up_s.shape[0]
    sub = units // 4
    rows, width = own_ref.shape
    tiles = sgo_ref.shape[0]
    for q in range(4):
        up_s[q * sub : (q + 1) * sub] = ups[q][...]
        dn_s[q * sub : (q + 1) * sub] = downs[q][...]
    up = up_s[...]
    scale = 1.0 / (rows // tiles)
    reps = 128 // tiles
    pooled = []
    for n_ref, sg_ref, b in ((own_ref, sgo_ref, bo), (sib_ref, sgs_ref, bs)):
        sg = jnp.concatenate([sg_ref[...]] * reps, axis=0)
        dh = f32_dot(dn_s[...], sg, nt) * scale
        pool = jnp.zeros((units, 128), jnp.float32)
        for c in range(0, rows, 256):
            wide = min(256, rows - c)
            pre = f32_dot(up, n_ref[c : c + wide, :], nt)
            for q in range(0, wide, 128):
                w = min(128, wide - q)
                hid, slope = gelu_pair(pre[:, q : q + w])
                b[:, c + q : c + q + w] = (slope * dh[:, :w]).astype(jnp.bfloat16)
                if w < 128:
                    hid = jnp.concatenate([hid, jnp.zeros((units, 128 - w), jnp.float32)], axis=1)
                pool = pool + hid
        shift = 64
        while shift >= tiles:
            pool = pool + pltpu.roll(pool, shift, 1)
            shift //= 2
        pooled.append((pool * scale).astype(jnp.bfloat16))
    pick = (
        lax.broadcasted_iota(jnp.int32, (tiles, 128), 0)
        == lax.broadcasted_iota(jnp.int32, (tiles, 128), 1)
    ).astype(jnp.bfloat16)
    flat = [f32_dot(pick, p, nt).astype(jnp.bfloat16) for p in pooled]
    emb_out[...] = emb_ref[...] + f32_dot(jnp.concatenate(flat, axis=0), dn_s[...])
    pay_ref[0:units] = (f32_dot(bo[...], own_ref[...]) + f32_dot(bs[...], sib_ref[...])).astype(
        jnp.bfloat16
    )
    pay_ref[units : units + tiles] = sgo_ref[...]
    pay_ref[units + tiles : units + 2 * tiles] = sgs_ref[...]
    pay_ref[units + 2 * tiles : units + 3 * tiles, 0:units] = flat[0]
    pay_ref[units + 2 * tiles : units + 3 * tiles, units : 2 * units] = flat[1]


def hidden_block(starts, own, sib, sg_own, sg_sib, up_weight, down_weight, emb):
    rows, width = own.shape
    tiles = sg_own.shape[0]
    units = up_weight.shape[0] // 8
    sub = units // 4
    whole = lambda shape: pl.BlockSpec(shape, lambda i, s: (0, 0))
    part = lambda q: pl.BlockSpec((sub, width), lambda i, s: (s[q], 0))
    return pl.pallas_call(
        block_kernel,
        out_shape=(
            jax.ShapeDtypeStruct((units + 3 * tiles, width), jnp.bfloat16),
            jax.ShapeDtypeStruct((2 * tiles, width), jnp.float32),
        ),
        grid_spec=pltpu.PrefetchScalarGridSpec(
            num_scalar_prefetch=1,
            grid=(1,),
            in_specs=[whole((rows, width))] * 2
            + [whole((tiles, width))] * 2
            + [part(q) for q in range(4)] * 2
            + [whole((2 * tiles, width))],
            out_specs=(whole((units + 3 * tiles, width)), whole((2 * tiles, width))),
            scratch_shapes=[
                pltpu.VMEM((units, width), jnp.bfloat16),
                pltpu.VMEM((units, width), jnp.bfloat16),
                pltpu.VMEM((units, rows), jnp.bfloat16),
                pltpu.VMEM((units, rows), jnp.bfloat16),
            ],
        ),
        compiler_params=pltpu.CompilerParams(vmem_limit_bytes=40 << 20),
        cost_estimate=pl.CostEstimate(
            flops=8_000_000_000, bytes_accessed=7_000_000, transcendentals=0
        ),
        name="hidden_block",
    )(starts, own, sib, sg_own, sg_sib, *([up_weight] * 4), *([down_weight] * 4), emb)


def combine_kernel(a_ref, b_ref, c_ref, d_ref, *outs):
    units = outs[0].shape[0] * 4
    width = a_ref.shape[1]
    tiles = (a_ref.shape[0] - units) // 3
    refs = (a_ref, b_ref, c_ref, d_ref)
    up = None
    for r in refs:
        term = r[0:units].astype(jnp.float32)
        up = term if up is None else up + term
    sg = jnp.concatenate([r[units : units + 2 * tiles] for r in refs], axis=0)
    low, high = units + 2 * tiles, units + 3 * tiles
    pool = jnp.concatenate(
        [r[low:high, h * units : (h + 1) * units] for r in refs for h in range(2)], axis=0
    )
    down = f32_dot(pool, sg, tn)
    sub = units // 4
    for q, out in enumerate(outs):
        out[:, 0:width] = up[q * sub : (q + 1) * sub].astype(jnp.bfloat16)
        out[:, width : 2 * width] = down[q * sub : (q + 1) * sub].astype(jnp.bfloat16)


def combine(payloads, units):
    width = payloads[0].shape[1]
    shape = jax.ShapeDtypeStruct((units // 4, 2 * width), jnp.bfloat16)
    return pl.pallas_call(
        combine_kernel,
        out_shape=(shape,) * 4,
        in_specs=[VMEM] * 4,
        out_specs=(VMEM,) * 4,
        compiler_params=pltpu.CompilerParams(vmem_limit_bytes=24 << 20),
        cost_estimate=pl.CostEstimate(
            flops=400_000_000, bytes_accessed=4_000_000, transcendentals=0
        ),
        name="combine",
    )(*payloads)


def move(value, stage, hop):
    pairs = []
    for x in range(4):
        for c in range(2):
            for y in range(4):
                for z in range(4):
                    to = [x, c, y, z]
                    if stage == 0:
                        to[1] = 1 - c
                    else:
                        spot = 3 if stage == 3 else (0 if (stage == 1) == (c == 0) else 2)
                        to[spot] = (to[spot] + hop) % 4
                    line = lambda p: (p[0] * 2 + p[1]) * 16 + p[2] * 4 + p[3]
                    pairs.append((line((x, c, y, z)), line(to)))
    return lax.ppermute(value, axes, pairs)


def slot_table(owners, own_count, owner_total, capacity):
    slot_total = owners.shape[0]
    slots = jnp.arange(slot_total, dtype=jnp.int32)
    live = slots < own_count
    same = (owners[:, None] == owners[None, :]) & (slots[None, :] < slots[:, None])
    rank = jnp.sum(same.astype(jnp.int32), axis=1, dtype=jnp.int32)
    target = rank * owner_total + owners
    chosen = (
        target[:, None] == jnp.arange(owner_total * capacity, dtype=jnp.int32)[None, :]
    ) & live[:, None]
    return chosen.astype(jnp.bfloat16)


def body(tile_maps, tile_owner, tissue_counts, embed_grad, depth_kernel, up_weight, down_weight):
    lane_count = lax.axis_size("enc")
    slide, enc = lax.axis_index("slide"), lax.axis_index("enc")
    x, core, y, z = slide // 2, slide % 2, enc // 4, enc % 4
    first = jnp.where(core == 0, x, y)
    second = jnp.where(core == 0, y, x)

    maps = jnp.transpose(tile_maps[0], (1, 2, 0, 3))
    tiles, width = maps.shape[2:]
    hidden = up_weight.shape[0]
    units = hidden // 8
    sub = units // 4
    owners = tile_owner.reshape(tiles)
    row_counts = tissue_counts.reshape(lane_count)
    own_count = jnp.sum(
        jnp.where(jnp.arange(lane_count, dtype=jnp.int32) == enc, row_counts, 0), dtype=jnp.int32
    )
    capacity = embed_grad.shape[3]
    table = slot_table(owners, own_count, lane_count, capacity)

    fetched = lax.all_to_all(
        jnp.transpose(embed_grad[0, 0], (1, 0, 2)), "enc", split_axis=1, concat_axis=1, tiled=True
    )
    slot_grad = f32_dot(table, fetched.reshape(capacity * lane_count, width)).astype(jnp.bfloat16)
    sib_grad = move(slot_grad, 0, 0)

    normed, map_mean = conv_norm(maps, depth_kernel)
    normed = normed.reshape(-1, width)
    sib_normed = move(normed, 0, 0)

    emb = jnp.zeros((2 * tiles, width), jnp.float32)
    payloads = []
    for hop in hops + (0,):
        goal = (first + hop) % 4
        inner = (second + jnp.arange(1, 5, dtype=jnp.int32)) % 4
        goal_x = jnp.where(core == 0, goal, inner)
        goal_y = jnp.where(core == 0, inner, goal)
        starts = ((2 * goal_x + core) * 4 + goal_y).astype(jnp.int32)
        pay, emb = hidden_block(
            starts, normed, sib_normed, slot_grad, sib_grad, up_weight, down_weight, emb
        )
        payloads.append(move(pay, 1, hop) if hop else pay)

    tile_embed = (map_mean + emb[:tiles] + move(emb[tiles:], 0, 0)).astype(jnp.bfloat16)
    outgoing = f32_dot(table, tile_embed, tn).astype(jnp.bfloat16)
    arrived = lax.all_to_all(
        outgoing.reshape(capacity, lane_count, width), "enc", split_axis=1, concat_axis=1, tiled=True
    )
    slide_embed = jnp.transpose(arrived, (1, 0, 2))[None, None]

    parts = combine(payloads, units)
    mine = parts[3].astype(jnp.float32)
    for hop in (1, 2, 3):
        mine = mine + move(parts[hop - 1], 2, hop).astype(jnp.float32)
    last = sub // 4
    pick = lambda hop: lax.dynamic_slice_in_dim(mine, ((z + hop) % 4) * last, last, 0)
    total = pick(0)
    for hop in (1, 2, 3):
        total = total + move(pick(hop).astype(jnp.bfloat16), 3, hop).astype(jnp.float32)
    return slide_embed, total[:, :width], total[:, width:]


def solution(mesh):
    in_specs = (
        P("slide", "enc", None, None, None),
        P("slide", "enc", None),
        P("slide", None),
        P("slide", "enc", None, None, None),
        P(),
        P(),
        P(),
    )
    out_specs = (
        P("slide", "enc", None, None, None),
        P(("slide", "enc"), None),
        P(("slide", "enc"), None),
    )
    return jax.shard_map(body, mesh=mesh, in_specs=in_specs, out_specs=out_specs, check_vma=False)
```

```python
import functools

import jax
import jax.numpy as jnp
from jax import lax
from jax.experimental import pallas as pl
from jax.experimental.pallas import tpu as pltpu
from jax.sharding import PartitionSpec as P

root_half = 0.7071067811865476
half_log2_e = -0.7213475204444817
log2_inv_root_two_pi = -1.3257480647361592
axes = ("slide", "enc")
hops = (2, 1, 3)
VMEM = pl.BlockSpec(memory_space=pltpu.VMEM)
SMEM = pl.BlockSpec(memory_space=pltpu.SMEM)
small_cost = pl.CostEstimate(flops=1000, bytes_accessed=1000, transcendentals=0)
nt = (((1,), (1,)), ((), ()))
tn = (((0,), (0,)), ((), ()))


def f32_dot(lhs, rhs, dims=(((1,), (0,)), ((), ()))):
    return lax.dot_general(lhs, rhs, dims, preferred_element_type=jnp.float32)


def conv_kernel(low, high, x_ref, k_ref, normed_ref, *rest):
    xf, kf, cv = rest[-3:]
    means = rest[:-3]
    side = x_ref.shape[0]
    tiles, width = x_ref.shape[2:]
    cells, reach = side * side, side // 2
    seen = range(max(0, low - reach) * side, cells)
    for n in range(cells):
        kf[n] = jnp.broadcast_to(
            k_ref[n // side, n % side : n % side + 1].astype(jnp.float32), (8, width)
        )

    @pl.loop(0, tiles // 16)
    def _(group):
        row = pl.multiple_of(group * 16, 16)
        for n in range(cells) if means else seen:
            xf[n] = x_ref[n // side, n % side, pl.ds(row, 16), :].astype(jnp.float32)

        @pl.loop(0, 2 * (width // 128))
        def _(unit):
            lane = pl.multiple_of((unit // 2) * 128, 128)
            half = pl.multiple_of((unit % 2) * 8, 8)
            for i in range(low, high):
                acc = [None] * side
                for a in range(side):
                    r = i + a - reach
                    if not 0 <= r < side:
                        continue
                    xs = [xf[r * side + j, pl.ds(half, 8), pl.ds(lane, 128)] for j in range(side)]
                    ks = [kf[a * side + b, :, pl.ds(lane, 128)] for b in range(side)]
                    for j in range(side):
                        for b in range(side):
                            c = j + b - reach
                            if 0 <= c < side:
                                term = xs[c] * ks[b]
                                acc[j] = term if acc[j] is None else acc[j] + term
                for j in range(side):
                    cv[(i - low) * side + j, pl.ds(half, 8), pl.ds(lane, 128)] = acc[j]

        for n in range((high - low) * side):
            conv = cv[n]
            centred = conv - jnp.sum(conv, axis=1, keepdims=True) * (1.0 / width)
            var = jnp.sum(centred * centred, axis=1, keepdims=True) * (1.0 / width)
            normed_ref[n, pl.ds(row, 16), :] = (centred * lax.rsqrt(var + 1e-6)).astype(jnp.bfloat16)
        for mean_ref in means:
            total = xf[0]
            for n in range(1, cells):
                total = total + xf[n]
            mean_ref[pl.ds(row, 16), :] = total * (1.0 / cells)


def conv_norm(maps, kernel, low, high, with_mean):
    side, _, tiles, width = maps.shape
    cells = (high - low) * side
    return pl.pallas_call(
        functools.partial(conv_kernel, low, high),
        out_shape=(
            jax.ShapeDtypeStruct((cells, tiles, width), jnp.bfloat16),
            *[jax.ShapeDtypeStruct((tiles, width), jnp.float32)] * with_mean,
        ),
        in_specs=[VMEM] * 2,
        out_specs=(VMEM,) * (1 + with_mean),
        scratch_shapes=[
            pltpu.VMEM((side * side, 16, width), jnp.float32),
            pltpu.VMEM((side * side, 8, width), jnp.float32),
            pltpu.VMEM((cells, 16, width), jnp.float32),
        ],
        compiler_params=pltpu.CompilerParams(vmem_limit_bytes=16 << 20),
        cost_estimate=small_cost,
        name="conv_norm",
    )(maps, kernel)


def gelu_pair(pre):
    cdf = 0.5 + 0.5 * lax.erf(pre * root_half)
    density = jnp.exp2(pre * pre * half_log2_e + log2_inv_root_two_pi)
    return pre * cdf, cdf + pre * density


def block_kernel(starts, *rest):
    parts, sgs = rest[0:4], rest[4:6]
    up_ref, down_ref, emb_ref, pay_ref, emb_out, up_s, dn_s, grads = rest[6:]
    units = up_s.shape[0]
    sub = units // 4
    width = up_ref.shape[1]
    tiles = sgs[0].shape[0]
    scale = 1.0 / ((parts[0].shape[0] + parts[1].shape[0]) // tiles)
    for q in range(4):
        rows = pl.ds(pl.multiple_of(starts[q] * sub, sub), sub)
        up_s[q * sub : (q + 1) * sub] = up_ref[rows, :]
        dn_s[q * sub : (q + 1) * sub] = down_ref[rows, :]
    up = up_s[...]
    both = jnp.concatenate([sg[...] for sg in sgs for _ in range(128 // tiles)], axis=0)
    dh_both = f32_dot(dn_s[...], both, nt) * scale
    dh = [dh_both[:, 0:128], dh_both[:, 128:256]]

    runs, tails = [], []
    for p, ref in enumerate(parts):
        full = ref.shape[0] // 256 * 256
        runs.append((p, full))
        for cut in range(full, ref.shape[0], 128):
            tails.append((p, cut, min(128, ref.shape[0] - cut)))
    tails.sort(key=lambda t: -t[2])
    pool = [jnp.zeros((units, 128), jnp.float32) for _ in range(2)]
    column = 0

    def tile(rhs, owners, column):
        pre = f32_dot(up, rhs, nt)
        at = 0
        for who, w in owners:
            hid, slope = gelu_pair(pre[:, at : at + w])
            grads[:, column + at : column + at + w] = (slope * dh[who][:, 0:w]).astype(jnp.bfloat16)
            if w < 128:
                hid = jnp.concatenate([hid, jnp.zeros((units, 128 - w), jnp.float32)], axis=1)
            pool[who] = pool[who] + hid
            at += w

    up_rows, waiting = None, None

    def absorb(todo, up_rows):
        start, size, rhs = todo
        term = f32_dot(grads[:, start : start + size], rhs())
        return term if up_rows is None else up_rows + term

    for p, full in runs:
        start = column
        for cut in range(0, full, 256):
            tile(parts[p][cut : cut + 256, :], [(p // 2, 128)] * 2, column)
            column += 256
        if waiting is not None:
            up_rows = absorb(waiting, up_rows)
        waiting = (start, full, lambda p=p, full=full: parts[p][0:full, :])
    start = column
    group, size = [], 0
    for n, (p, cut, w) in enumerate(tails):
        group.append((p, cut, w))
        size += w
        if size == 256 or n == len(tails) - 1:
            rhs = jnp.concatenate([parts[q][c : c + v, :] for q, c, v in group], axis=0)
            tile(rhs, [(q // 2, v) for q, _, v in group], column)
            column += size
            group, size = [], 0
    up_rows = absorb(waiting, up_rows)
    rhs = jnp.concatenate([parts[p][c : c + w, :] for p, c, w in tails], axis=0)
    up_rows = absorb((start, column - start, lambda: rhs), up_rows)
    pay_ref[0:units] = up_rows.astype(jnp.bfloat16)

    pick = (
        lax.broadcasted_iota(jnp.int32, (tiles, 128), 0)
        == lax.broadcasted_iota(jnp.int32, (tiles, 128), 1)
    ).astype(jnp.bfloat16)
    flat = []
    for value in pool:
        shift = 64
        while shift >= tiles:
            value = value + pltpu.roll(value, shift, 1)
            shift //= 2
        flat.append(f32_dot(pick, (value * scale).astype(jnp.bfloat16), nt).astype(jnp.bfloat16))
    emb_out[...] = emb_ref[...] + f32_dot(jnp.concatenate(flat, axis=0), dn_s[...])
    for h in range(2):
        pay_ref[units + h * tiles : units + (h + 1) * tiles] = sgs[h][...]
        pay_ref[units + 2 * tiles : units + 3 * tiles, h * units : (h + 1) * units] = flat[h]


def hidden_block(starts, parts, grads, up_weight, down_weight, emb):
    tiles, width = grads[0].shape
    units = up_weight.shape[0] // 8
    rows = sum(p.shape[0] for p in parts)
    return pl.pallas_call(
        block_kernel,
        out_shape=(
            jax.ShapeDtypeStruct((units + 3 * tiles, width), jnp.bfloat16),
            jax.ShapeDtypeStruct((2 * tiles, width), jnp.float32),
        ),
        in_specs=[SMEM] + [VMEM] * 9,
        out_specs=(VMEM, VMEM),
        scratch_shapes=[
            pltpu.VMEM((units, width), jnp.bfloat16),
            pltpu.VMEM((units, width), jnp.bfloat16),
            pltpu.VMEM((units, rows), jnp.bfloat16),
        ],
        compiler_params=pltpu.CompilerParams(vmem_limit_bytes=24 << 20),
        cost_estimate=small_cost,
        name="hidden_block",
    )(starts, *parts, *grads, up_weight, down_weight, emb)


def combine_kernel(a_ref, b_ref, c_ref, d_ref, *outs):
    units = outs[0].shape[0] * 4
    width = a_ref.shape[1]
    tiles = (a_ref.shape[0] - units) // 3
    refs = (a_ref, b_ref, c_ref, d_ref)
    up = None
    for r in refs:
        term = r[0:units].astype(jnp.float32)
        up = term if up is None else up + term
    sg = jnp.concatenate([r[units : units + 2 * tiles] for r in refs], axis=0)
    low, high = units + 2 * tiles, units + 3 * tiles
    pool = jnp.concatenate(
        [r[low:high, h * units : (h + 1) * units] for r in refs for h in range(2)], axis=0
    )
    down = f32_dot(pool, sg, tn)
    sub = units // 4
    for q, out in enumerate(outs):
        out[:, 0:width] = up[q * sub : (q + 1) * sub].astype(out.dtype)
        out[:, width : 2 * width] = down[q * sub : (q + 1) * sub].astype(out.dtype)


def combine(payloads, units):
    width = payloads[0].shape[1]
    shape = lambda dtype: jax.ShapeDtypeStruct((units // 4, 2 * width), dtype)
    return pl.pallas_call(
        combine_kernel,
        out_shape=(shape(jnp.bfloat16),) * 3 + (shape(jnp.float32),),
        in_specs=[VMEM] * 4,
        out_specs=(VMEM,) * 4,
        compiler_params=pltpu.CompilerParams(vmem_limit_bytes=16 << 20),
        cost_estimate=small_cost,
        name="combine",
    )(*payloads)


def embed_kernel(table_ref, mean_ref, emb_ref, other_ref, *outs):
    tiles = mean_ref.shape[0]
    embed = (mean_ref[...] + emb_ref[0:tiles] + other_ref[...]).astype(jnp.bfloat16)
    sorted_rows = f32_dot(table_ref[...], embed, tn).astype(jnp.bfloat16)
    for k, out in enumerate(outs):
        out[...] = sorted_rows[16 * k : 16 * k + 16]


def embed_rows(table, mean, emb, other):
    width = mean.shape[1]
    return pl.pallas_call(
        embed_kernel,
        out_shape=(jax.ShapeDtypeStruct((16, width), jnp.bfloat16),) * 4,
        in_specs=[VMEM] * 4,
        out_specs=(VMEM,) * 4,
        cost_estimate=small_cost,
        name="embed_rows",
    )(table, mean, emb, other)


def second_kernel(z_ref, own_ref, *rest):
    received, embeds = rest[0:3], rest[3:7]
    own_out, pays, embed_out, total = rest[7], rest[8:11], rest[11], rest[12]
    width = own_out.shape[1]
    last = own_ref.shape[0] // 4
    total[...] = own_ref[...] + sum(r[...].astype(jnp.float32) for r in received)
    row = lax.broadcasted_iota(jnp.int32, (64, 64), 0)
    col = lax.broadcasted_iota(jnp.int32, (64, 64), 1)
    match = None
    for j in range(4):
        for k in range(4):
            rank = row - (16 * j + 3 * k)
            hit = (rank >= 0) & (rank < 3) & (col == 16 * k + 3 * j + rank)
            match = hit if match is None else match | hit
    embeds = jnp.concatenate([e[...] for e in embeds], axis=0)
    embeds = f32_dot(match.astype(jnp.bfloat16), embeds)
    for j in range(4):
        rows = pl.ds(pl.multiple_of(lax.rem(z_ref[0] + j, 4) * last, 8), last)
        up, down = total[rows, 0:width], total[rows, width : 2 * width]
        if j == 0:
            own_out[...] = jnp.concatenate([up, down], axis=0)
            embed_out[...] = embeds[0:16].astype(jnp.bfloat16)
        else:
            pays[j - 1][...] = jnp.concatenate(
                [up, down, embeds[16 * j : 16 * j + 16]], axis=0
            ).astype(jnp.bfloat16)


def second_sum(z, own, received, embeds):
    sub, width = own.shape[0], own.shape[1] // 2
    rows = sub // 2
    return pl.pallas_call(
        second_kernel,
        out_shape=(
            jax.ShapeDtypeStruct((rows, width), jnp.float32),
            *[jax.ShapeDtypeStruct((rows + 16, width), jnp.bfloat16)] * 3,
            jax.ShapeDtypeStruct((16, width), jnp.bfloat16),
        ),
        in_specs=[SMEM] + [VMEM] * 8,
        out_specs=(VMEM,) * 5,
        scratch_shapes=[pltpu.VMEM(own.shape, jnp.float32)],
        cost_estimate=small_cost,
        name="second_sum",
    )(z, own, *received, *embeds)


def last_kernel(place_ref, own_ref, embed_ref, a_ref, b_ref, c_ref, up_ref, down_ref, out_ref):
    half = up_ref.shape[0]
    rows = 2 * half
    total = own_ref[...]
    for r in (a_ref, b_ref, c_ref):
        total = total + r[...].astype(jnp.float32)[0:rows]
    up_ref[...] = total[0:half]
    down_ref[...] = total[half:rows]
    embeds = jnp.concatenate(
        [embed_ref[...]] + [r[rows : rows + 16] for r in (a_ref, b_ref, c_ref)], axis=0
    )
    out_ref[...] = f32_dot(place_ref[...], embeds).astype(jnp.bfloat16)


def last_sum(place, own, embed, received):
    rows, width = own.shape
    return pl.pallas_call(
        last_kernel,
        out_shape=(
            jax.ShapeDtypeStruct((rows // 2, width), jnp.float32),
            jax.ShapeDtypeStruct((rows // 2, width), jnp.float32),
            jax.ShapeDtypeStruct((place.shape[0], width), jnp.bfloat16),
        ),
        in_specs=[VMEM] * 6,
        out_specs=(VMEM,) * 3,
        cost_estimate=small_cost,
        name="last_sum",
    )(place, own, embed, *received)


def move(value, stage, hop):
    pairs = []
    for x in range(4):
        for c in range(2):
            for y in range(4):
                for z in range(4):
                    to = [x, c, y, z]
                    if stage == 0:
                        to[1] = 1 - c
                    else:
                        spot = {1: 2 * c, 2: 2 - 2 * c, 3: 3, 4: 2}[stage]
                        to[spot] = (to[spot] + hop) % 4
                    line = lambda p: (p[0] * 2 + p[1]) * 16 + p[2] * 4 + p[3]
                    pairs.append((line((x, c, y, z)), line(to)))
    return lax.ppermute(value, axes, pairs)


def one_hot(index, size, live):
    hit = index[:, None] == jnp.arange(size, dtype=jnp.int32)[None, :]
    return (hit & live[:, None]).astype(jnp.bfloat16)


def body(tile_maps, tile_owner, tissue_counts, embed_grad, depth_kernel, up_weight, down_weight):
    lane_count = lax.axis_size("enc")
    slide, enc = lax.axis_index("slide"), lax.axis_index("enc")
    x, core, y, z = slide // 2, slide % 2, enc // 4, enc % 4
    first = jnp.where(core == 0, x, y)
    second = jnp.where(core == 0, y, x)

    maps = jnp.transpose(tile_maps[0], (1, 2, 0, 3))
    side, _, tiles, width = maps.shape
    units = up_weight.shape[0] // 8
    capacity = embed_grad.shape[3]

    fetched = lax.all_to_all(
        jnp.transpose(embed_grad[0, 0], (1, 0, 2)), "enc", split_axis=1, concat_axis=1, tiled=True
    )

    owners = tile_owner.reshape(tiles)
    row_counts = tissue_counts.reshape(lane_count)
    own_count = jnp.sum(
        jnp.where(jnp.arange(lane_count, dtype=jnp.int32) == enc, row_counts, 0), dtype=jnp.int32
    )
    slots = jnp.arange(tiles, dtype=jnp.int32)
    live = slots < own_count
    same = (owners[:, None] == owners[None, :]) & (slots[None, :] < slots[:, None])
    rank = jnp.sum(same.astype(jnp.int32), axis=1, dtype=jnp.int32)
    table = one_hot(rank * lane_count + owners, lane_count * capacity, live)
    hops_y, hops_z = (owners // 4 - y) % 4, (owners % 4 - z) % 4
    send_table = one_hot(hops_y * 16 + hops_z * 3 + rank, 64, live)
    spots = jnp.arange(capacity * lane_count, dtype=jnp.int32)
    reader = spots % lane_count
    from_y, from_z = (y - reader // 4) % 4, (z - reader % 4) % 4
    place = one_hot(from_z * 16 + from_y * 3 + spots // lane_count, 64, spots >= 0)

    half = side // 2 + 1
    (normed_a,) = conv_norm(maps, depth_kernel, 0, half, 0)
    normed_a = normed_a.reshape(-1, width)
    sib_a = move(normed_a, 0, 0)

    slot_grad = f32_dot(table, fetched.reshape(capacity * lane_count, width)).astype(jnp.bfloat16)
    sib_grad = move(slot_grad, 0, 0)

    normed_b, map_mean = conv_norm(maps, depth_kernel, half, side, 1)
    normed_b = normed_b.reshape(-1, width)
    sib_b = move(normed_b, 0, 0)

    emb = jnp.zeros((2 * tiles, width), jnp.float32)
    payloads = []
    for hop in hops + (0,):
        goal = (first + hop) % 4
        inner = (second + jnp.arange(1, 5, dtype=jnp.int32)) % 4
        goal_x = jnp.where(core == 0, goal, inner)
        goal_y = jnp.where(core == 0, inner, goal)
        starts = ((2 * goal_x + core) * 4 + goal_y).astype(jnp.int32)
        if not hop:
            emb, payloads[0] = lax.optimization_barrier((emb, payloads[0]))
        pay, emb = hidden_block(
            starts,
            (normed_a, normed_b, sib_a, sib_b),
            (slot_grad, sib_grad),
            up_weight,
            down_weight,
            emb,
        )
        payloads.append(move(pay, 1, hop) if hop else pay)

    other_emb = move(emb[tiles:], 0, 0)
    other_emb, payloads[1] = lax.optimization_barrier((other_emb, payloads[1]))
    rows_out = embed_rows(send_table, map_mean, emb, other_emb)
    embeds = (rows_out[0],) + tuple(move(rows_out[hop], 4, hop) for hop in (1, 2, 3))
    payloads, embeds = lax.optimization_barrier((tuple(payloads), embeds))

    parts = combine(payloads, units)
    received = [move(parts[hop - 1], 2, hop) for hop in (1, 2, 3)]
    own, *pays, own_embed = second_sum(
        z.astype(jnp.int32).reshape(1), parts[3], received, embeds
    )
    received = [move(pays[hop - 1], 3, hop) for hop in (1, 2, 3)]
    up_part, down_part, arrived = last_sum(place, own, own_embed, received)
    slide_embed = jnp.transpose(arrived.reshape(capacity, lane_count, width), (1, 0, 2))
    return slide_embed[None, None], up_part, down_part


def solution(mesh):
    in_specs = (
        P("slide", "enc", None, None, None),
        P("slide", "enc", None),
        P("slide", None),
        P("slide", "enc", None, None, None),
        P(),
        P(),
        P(),
    )
    out_specs = (
        P("slide", "enc", None, None, None),
        P(("slide", "enc"), None),
        P(("slide", "enc"), None),
    )
    return jax.shard_map(body, mesh=mesh, in_specs=in_specs, out_specs=out_specs, check_vma=False)
```

```python
import functools

import jax
import jax.numpy as jnp
from jax import lax
from jax.experimental import pallas as pl
from jax.experimental.pallas import tpu as pltpu
from jax.sharding import PartitionSpec as P

root_half = 0.7071067811865476
half_log2_e = -0.7213475204444817
log2_inv_root_two_pi = -1.3257480647361592
axes = ("slide", "enc")
hops = (2, 1, 3)
VMEM = pl.BlockSpec(memory_space=pltpu.VMEM)
SMEM = pl.BlockSpec(memory_space=pltpu.SMEM)
HBM = pl.BlockSpec(memory_space=pltpu.HBM)
small_cost = pl.CostEstimate(flops=1000, bytes_accessed=1000, transcendentals=0)
nt = (((1,), (1,)), ((), ()))
tn = (((0,), (0,)), ((), ()))


def f32_dot(lhs, rhs, dims=(((1,), (0,)), ((), ()))):
    return lax.dot_general(lhs, rhs, dims, preferred_element_type=jnp.float32)


def row_hits(index, size):
    return index == lax.broadcasted_iota(jnp.int32, (index.shape[0], size), 1)


def slot_tables(here_ref, column_ref, line_ref, table_ref, send_ref, place_ref):
    count, y, z = here_ref[16], here_ref[17], here_ref[18]
    tiles = column_ref.shape[0]
    lanes = 16
    owners = column_ref[...]
    slot = lax.broadcasted_iota(jnp.int32, (tiles, tiles), 0)
    other = lax.broadcasted_iota(jnp.int32, (tiles, tiles), 1)
    same = jnp.where((owners == line_ref[...]) & (other < slot), 1.0, 0.0)
    rank = jnp.sum(same, axis=1, keepdims=True).astype(jnp.int32)
    live = lax.broadcasted_iota(jnp.int32, (tiles, 1), 0) < count
    pick = lambda index, size, on: jnp.where(row_hits(index, size) & on, 1.0, 0.0).astype(jnp.bfloat16)
    table_ref[...] = pick(rank * lanes + owners, table_ref.shape[1], live)
    hops_y, hops_z = ((owners >> 2) - y) & 3, ((owners & 3) - z) & 3
    send_ref[...] = pick(hops_y * 16 + hops_z * 3 + rank, send_ref.shape[1], live)
    spots = lax.broadcasted_iota(jnp.int32, (place_ref.shape[0], 1), 0)
    reader = spots & (lanes - 1)
    from_y, from_z = (y - (reader >> 2)) & 3, (z - (reader & 3)) & 3
    place_ref[...] = pick(from_z * 16 + from_y * 3 + (spots >> 4), place_ref.shape[1], spots >= 0)


def conv_kernel(here_ref, column_ref, line_ref, x_hbm, k_hbm, up_hbm, down_hbm, *rest):
    normed_ref, mean_ref, table_ref, send_ref, place_ref = rest[0:5]
    weights = rest[5:13]
    xb, kb, xf, kf, cv, sems = rest[13:]
    side = kb.shape[0]
    tiles, width = mean_ref.shape
    cells, reach = side * side, side // 2
    units = weights[0].shape[0]
    sub = units // 4

    def maps_copy(group):
        rows = pl.ds(group * 16, 16)
        return pltpu.make_async_copy(x_hbm.at[:, :, rows, :], xb.at[group], sems.at[group])

    def weight_copy(n):
        start = pl.ds(pl.multiple_of(here_ref[n % 16] * sub, sub), sub)
        source = (up_hbm if n < 16 else down_hbm).at[start, :]
        goal = weights[n // 4].at[pl.ds(n % 4 * sub, sub), :]
        return pltpu.make_async_copy(source, goal, sems.at[3 + n])

    kernel_copy = pltpu.make_async_copy(k_hbm, kb, sems.at[2])
    kernel_copy.start()
    for group in range(tiles // 16):
        maps_copy(group).start()
    for n in range(32):
        weight_copy(n).start()
    slot_tables(here_ref, column_ref, line_ref, table_ref, send_ref, place_ref)
    kernel_copy.wait()
    for n in range(cells):
        kf[n] = jnp.broadcast_to(
            kb[n // side, n % side : n % side + 1].astype(jnp.float32), (8, width)
        )

    @pl.loop(0, tiles // 16)
    def _(group):
        row = pl.multiple_of(group * 16, 16)
        maps_copy(group).wait()
        for n in range(cells):
            xf[n] = xb[group, n // side, n % side].astype(jnp.float32)

        @pl.loop(0, 2 * (width // 128))
        def _(unit):
            lane = pl.multiple_of((unit // 2) * 128, 128)
            half = pl.multiple_of((unit % 2) * 8, 8)
            for i in range(side):
                acc = [None] * side
                for a in range(side):
                    r = i + a - reach
                    if not 0 <= r < side:
                        continue
                    xs = [xf[r * side + j, pl.ds(half, 8), pl.ds(lane, 128)] for j in range(side)]
                    ks = [kf[a * side + b, :, pl.ds(lane, 128)] for b in range(side)]
                    for j in range(side):
                        for b in range(side):
                            c = j + b - reach
                            if 0 <= c < side:
                                term = xs[c] * ks[b]
                                acc[j] = term if acc[j] is None else acc[j] + term
                for j in range(side):
                    cv[i * side + j, pl.ds(half, 8), pl.ds(lane, 128)] = acc[j]

        total = None
        for n in range(cells):
            conv = cv[n]
            centred = conv - jnp.sum(conv, axis=1, keepdims=True) * (1.0 / width)
            var = jnp.sum(centred * centred, axis=1, keepdims=True) * (1.0 / width)
            normed_ref[n, pl.ds(row, 16), :] = (centred * lax.rsqrt(var + 1e-6)).astype(jnp.bfloat16)
            total = xf[n] if total is None else total + xf[n]
        mean_ref[pl.ds(row, 16), :] = total * (1.0 / cells)

    for n in range(32):
        weight_copy(n).wait()


def conv_norm(here, owners, maps, kernel, up_weight, down_weight, capacity):
    side, _, tiles, width = maps.shape
    cells = side * side
    units = up_weight.shape[0] // 8
    shape = jax.ShapeDtypeStruct
    return pl.pallas_call(
        conv_kernel,
        out_shape=(
            shape((cells, tiles, width), jnp.bfloat16),
            shape((tiles, width), jnp.float32),
            shape((tiles, 16 * capacity), jnp.bfloat16),
            shape((tiles, 64), jnp.bfloat16),
            shape((16 * capacity, 64), jnp.bfloat16),
            *[shape((units, width), jnp.bfloat16)] * 8,
        ),
        in_specs=[SMEM] + [VMEM] * 2 + [HBM] * 4,
        out_specs=(VMEM,) * 5 + (HBM,) * 8,
        scratch_shapes=[
            pltpu.VMEM((tiles // 16, side, side, 16, width), jnp.bfloat16),
            pltpu.VMEM(kernel.shape, jnp.bfloat16),
            pltpu.VMEM((cells, 16, width), jnp.float32),
            pltpu.VMEM((cells, 8, width), jnp.float32),
            pltpu.VMEM((cells, 16, width), jnp.float32),
            pltpu.SemaphoreType.DMA((35,)),
        ],
        compiler_params=pltpu.CompilerParams(vmem_limit_bytes=50 << 20),
        cost_estimate=small_cost,
        name="conv_norm",
    )(here, owners.reshape(tiles, 1), owners.reshape(1, tiles), maps, kernel, up_weight, down_weight)


def gelu_pair(pre):
    cdf = 0.5 + 0.5 * lax.erf(pre * root_half)
    density = jnp.exp2(pre * pre * half_log2_e + log2_inv_root_two_pi)
    return pre * cdf, cdf + pre * density


def block_kernel(*rest):
    parts, sgs = rest[0:2], rest[2:4]
    up_s, dn_s, emb_ref, pay_ref, emb_out, grads = rest[4:]
    units = up_s.shape[0]
    tiles = sgs[0].shape[0]
    scale = 1.0 / (parts[0].shape[0] // tiles)
    up = up_s[...]
    both = jnp.concatenate([sg[...] for sg in sgs for _ in range(128 // tiles)], axis=0)
    dh_both = f32_dot(dn_s[...], both, nt) * scale
    dh = [dh_both[:, 0:128], dh_both[:, 128:256]]

    runs, tails = [], []
    for p, ref in enumerate(parts):
        full = ref.shape[0] // 256 * 256
        runs.append((p, full))
        for cut in range(full, ref.shape[0], 128):
            tails.append((p, cut, min(128, ref.shape[0] - cut)))
    tails.sort(key=lambda t: -t[2])
    pool = [jnp.zeros((units, 128), jnp.float32) for _ in range(2)]
    column = 0

    def tile(rhs, owners, column):
        pre = f32_dot(up, rhs, nt)
        at = 0
        for who, w in owners:
            hid, slope = gelu_pair(pre[:, at : at + w])
            grads[:, column + at : column + at + w] = (slope * dh[who][:, 0:w]).astype(jnp.bfloat16)
            if w < 128:
                hid = jnp.concatenate([hid, jnp.zeros((units, 128 - w), jnp.float32)], axis=1)
            pool[who] = pool[who] + hid
            at += w

    up_rows, waiting = None, None

    def absorb(todo, up_rows):
        start, size, rhs = todo
        term = f32_dot(grads[:, start : start + size], rhs())
        return term if up_rows is None else up_rows + term

    for p, full in runs:
        start = column
        for cut in range(0, full, 256):
            tile(parts[p][cut : cut + 256, :], [(p, 128)] * 2, column)
            column += 256
        if waiting is not None:
            up_rows = absorb(waiting, up_rows)
        waiting = (start, full, lambda p=p, full=full: parts[p][0:full, :])
    start = column
    group, size = [], 0
    for n, (p, cut, w) in enumerate(tails):
        group.append((p, cut, w))
        size += w
        if size == 256 or n == len(tails) - 1:
            rhs = jnp.concatenate([parts[q][c : c + v, :] for q, c, v in group], axis=0)
            tile(rhs, [(q, v) for q, _, v in group], column)
            column += size
            group, size = [], 0
    up_rows = absorb(waiting, up_rows)
    rhs = jnp.concatenate([parts[p][c : c + w, :] for p, c, w in tails], axis=0)
    up_rows = absorb((start, column - start, lambda: rhs), up_rows)
    pay_ref[0:units] = up_rows.astype(jnp.bfloat16)

    pick = (
        lax.broadcasted_iota(jnp.int32, (tiles, 128), 0)
        == lax.broadcasted_iota(jnp.int32, (tiles, 128), 1)
    ).astype(jnp.bfloat16)
    flat = []
    for value in pool:
        shift = 64
        while shift >= tiles:
            value = value + pltpu.roll(value, shift, 1)
            shift //= 2
        flat.append(f32_dot(pick, (value * scale).astype(jnp.bfloat16), nt).astype(jnp.bfloat16))
    emb_out[...] = emb_ref[...] + f32_dot(jnp.concatenate(flat, axis=0), dn_s[...])
    for h in range(2):
        pay_ref[units + h * tiles : units + (h + 1) * tiles] = sgs[h][...]
        pay_ref[units + 2 * tiles : units + 3 * tiles, h * units : (h + 1) * units] = flat[h]


def hidden_block(parts, grads, up, down, emb):
    tiles, width = grads[0].shape
    units = up.shape[0]
    rows = sum(p.shape[0] for p in parts)
    return pl.pallas_call(
        block_kernel,
        out_shape=(
            jax.ShapeDtypeStruct((units + 3 * tiles, width), jnp.bfloat16),
            jax.ShapeDtypeStruct((2 * tiles, width), jnp.float32),
        ),
        in_specs=[VMEM] * 7,
        out_specs=(VMEM, VMEM),
        scratch_shapes=[pltpu.VMEM((units, rows), jnp.bfloat16)],
        compiler_params=pltpu.CompilerParams(vmem_limit_bytes=16 << 20),
        cost_estimate=small_cost,
        name="hidden_block",
    )(*parts, *grads, up, down, emb)


def combine_kernel(a_ref, b_ref, c_ref, d_ref, *outs):
    units = outs[0].shape[0] * 4
    width = a_ref.shape[1]
    tiles = (a_ref.shape[0] - units) // 3
    refs = (a_ref, b_ref, c_ref, d_ref)
    up = None
    for r in refs:
        term = r[0:units].astype(jnp.float32)
        up = term if up is None else up + term
    sg = jnp.concatenate([r[units : units + 2 * tiles] for r in refs], axis=0)
    low, high = units + 2 * tiles, units + 3 * tiles
    pool = jnp.concatenate(
        [r[low:high, h * units : (h + 1) * units] for r in refs for h in range(2)], axis=0
    )
    down = f32_dot(pool, sg, tn)
    sub = units // 4
    for q, out in enumerate(outs):
        out[:, 0:width] = up[q * sub : (q + 1) * sub].astype(out.dtype)
        out[:, width : 2 * width] = down[q * sub : (q + 1) * sub].astype(out.dtype)


def combine(payloads, units):
    width = payloads[0].shape[1]
    shape = lambda dtype: jax.ShapeDtypeStruct((units // 4, 2 * width), dtype)
    return pl.pallas_call(
        combine_kernel,
        out_shape=(shape(jnp.bfloat16),) * 3 + (shape(jnp.float32),),
        in_specs=[VMEM] * 4,
        out_specs=(VMEM,) * 4,
        compiler_params=pltpu.CompilerParams(vmem_limit_bytes=16 << 20),
        cost_estimate=small_cost,
        name="combine",
    )(*payloads)


def embed_kernel(table_ref, mean_ref, emb_ref, other_ref, *outs):
    tiles = mean_ref.shape[0]
    embed = (mean_ref[...] + emb_ref[0:tiles] + other_ref[...]).astype(jnp.bfloat16)
    sorted_rows = f32_dot(table_ref[...], embed, tn).astype(jnp.bfloat16)
    for k, out in enumerate(outs):
        out[...] = sorted_rows[16 * k : 16 * k + 16]


def embed_rows(table, mean, emb, other):
    width = mean.shape[1]
    return pl.pallas_call(
        embed_kernel,
        out_shape=(jax.ShapeDtypeStruct((16, width), jnp.bfloat16),) * 4,
        in_specs=[VMEM] * 4,
        out_specs=(VMEM,) * 4,
        compiler_params=pltpu.CompilerParams(vmem_limit_bytes=4 << 20),
        cost_estimate=small_cost,
        name="embed_rows",
    )(table, mean, emb, other)


def second_kernel(z_ref, own_ref, *rest):
    received, embeds = rest[0:3], rest[3:7]
    own_out, pays, embed_out, total = rest[7], rest[8:11], rest[11], rest[12]
    width = own_out.shape[1]
    last = own_ref.shape[0] // 4
    total[...] = own_ref[...] + sum(r[...].astype(jnp.float32) for r in received)
    row = lax.broadcasted_iota(jnp.int32, (64, 64), 0)
    col = lax.broadcasted_iota(jnp.int32, (64, 64), 1)
    match = None
    for j in range(4):
        for k in range(4):
            rank = row - (16 * j + 3 * k)
            hit = (rank >= 0) & (rank < 3) & (col == 16 * k + 3 * j + rank)
            match = hit if match is None else match | hit
    embeds = jnp.concatenate([e[...] for e in embeds], axis=0)
    embeds = f32_dot(match.astype(jnp.bfloat16), embeds)
    for j in range(4):
        rows = pl.ds(pl.multiple_of(lax.rem(z_ref[0] + j, 4) * last, 8), last)
        up, down = total[rows, 0:width], total[rows, width : 2 * width]
        if j == 0:
            own_out[...] = jnp.concatenate([up, down], axis=0)
            embed_out[...] = embeds[0:16].astype(jnp.bfloat16)
        else:
            pays[j - 1][...] = jnp.concatenate(
                [up, down, embeds[16 * j : 16 * j + 16]], axis=0
            ).astype(jnp.bfloat16)


def second_sum(z, own, received, embeds):
    sub, width = own.shape[0], own.shape[1] // 2
    rows = sub // 2
    return pl.pallas_call(
        second_kernel,
        out_shape=(
            jax.ShapeDtypeStruct((rows, width), jnp.float32),
            *[jax.ShapeDtypeStruct((rows + 16, width), jnp.bfloat16)] * 3,
            jax.ShapeDtypeStruct((16, width), jnp.bfloat16),
        ),
        in_specs=[SMEM] + [VMEM] * 8,
        out_specs=(VMEM,) * 5,
        scratch_shapes=[pltpu.VMEM(own.shape, jnp.float32)],
        compiler_params=pltpu.CompilerParams(vmem_limit_bytes=8 << 20),
        cost_estimate=small_cost,
        name="second_sum",
    )(z, own, *received, *embeds)


def last_kernel(place_ref, own_ref, embed_ref, a_ref, b_ref, c_ref, up_ref, down_ref, out_ref):
    half = up_ref.shape[0]
    rows = 2 * half
    total = own_ref[...]
    for r in (a_ref, b_ref, c_ref):
        total = total + r[...].astype(jnp.float32)[0:rows]
    up_ref[...] = total[0:half]
    down_ref[...] = total[half:rows]
    embeds = jnp.concatenate(
        [embed_ref[...]] + [r[rows : rows + 16] for r in (a_ref, b_ref, c_ref)], axis=0
    )
    out_ref[...] = f32_dot(place_ref[...], embeds).astype(jnp.bfloat16)


def last_sum(place, own, embed, received):
    rows, width = own.shape
    return pl.pallas_call(
        last_kernel,
        out_shape=(
            jax.ShapeDtypeStruct((rows // 2, width), jnp.float32),
            jax.ShapeDtypeStruct((rows // 2, width), jnp.float32),
            jax.ShapeDtypeStruct((place.shape[0], width), jnp.bfloat16),
        ),
        in_specs=[VMEM] * 6,
        out_specs=(VMEM,) * 3,
        compiler_params=pltpu.CompilerParams(vmem_limit_bytes=4 << 20),
        cost_estimate=small_cost,
        name="last_sum",
    )(place, own, embed, *received)


def move(value, stage, hop):
    pairs = []
    for x in range(4):
        for c in range(2):
            for y in range(4):
                for z in range(4):
                    to = [x, c, y, z]
                    if stage == 0:
                        to[1] = 1 - c
                    else:
                        spot = {1: 2 * c, 2: 2 - 2 * c, 3: 3, 4: 2}[stage]
                        to[spot] = (to[spot] + hop) % 4
                    line = lambda p: (p[0] * 2 + p[1]) * 16 + p[2] * 4 + p[3]
                    pairs.append((line((x, c, y, z)), line(to)))
    return lax.ppermute(value, axes, pairs)


def body(tile_maps, tile_owner, tissue_counts, embed_grad, depth_kernel, up_weight, down_weight):
    lane_count = lax.axis_size("enc")
    slide, enc = lax.axis_index("slide"), lax.axis_index("enc")
    x, core, y, z = slide // 2, slide % 2, enc // 4, enc % 4
    first = jnp.where(core == 0, x, y)
    second = jnp.where(core == 0, y, x)

    maps = jnp.transpose(tile_maps[0], (1, 2, 0, 3))
    side, _, tiles, width = maps.shape
    units = up_weight.shape[0] // 8
    capacity = embed_grad.shape[3]

    fetched = lax.all_to_all(
        jnp.transpose(embed_grad[0, 0], (1, 0, 2)), "enc", split_axis=1, concat_axis=1, tiled=True
    )

    row_counts = tissue_counts.reshape(lane_count)
    own_count = jnp.sum(
        jnp.where(jnp.arange(lane_count, dtype=jnp.int32) == enc, row_counts, 0), dtype=jnp.int32
    )
    steps = jnp.arange(16, dtype=jnp.int32)
    order = jnp.where(steps < 4, 2, jnp.where(steps < 8, 1, jnp.where(steps < 12, 3, 0)))
    goal = (first + order) % 4
    inner = (second + steps + 1) % 4
    starts = jnp.where(
        core == 0, (2 * goal + core) * 4 + inner, (2 * inner + core) * 4 + goal
    )
    here = jnp.concatenate([starts.astype(jnp.int32), jnp.stack([own_count, y, z]).astype(jnp.int32)])
    normed, map_mean, table, send_table, place, *weights = conv_norm(
        here, tile_owner, maps, depth_kernel, up_weight, down_weight, capacity
    )
    normed = normed.reshape(-1, width)
    sib_normed = move(normed, 0, 0)

    slot_grad = f32_dot(table, fetched.reshape(capacity * lane_count, width)).astype(jnp.bfloat16)
    sib_grad = move(slot_grad, 0, 0)

    emb = jnp.zeros((2 * tiles, width), jnp.float32)
    payloads = []
    for n, hop in enumerate(hops + (0,)):
        if not hop:
            emb, payloads[0] = lax.optimization_barrier((emb, payloads[0]))
        pay, emb = hidden_block(
            (normed, sib_normed), (slot_grad, sib_grad), weights[n], weights[4 + n], emb
        )
        payloads.append(move(pay, 1, hop) if hop else pay)

    other_emb = move(emb[tiles:], 0, 0)
    payloads[1], payloads[3] = lax.optimization_barrier((payloads[1], payloads[3]))
    parts = combine(payloads, units)
    emb, parts = lax.optimization_barrier((emb, parts))
    rows_out = embed_rows(send_table, map_mean, emb, other_emb)
    embeds = (rows_out[0],) + tuple(move(rows_out[hop], 4, hop) for hop in (1, 2, 3))
    received = [move(parts[hop - 1], 2, hop) for hop in (1, 2, 3)]
    own, *pays, own_embed = second_sum(here[18:19], parts[3], received, embeds)
    received = [move(pays[hop - 1], 3, hop) for hop in (1, 2, 3)]
    up_part, down_part, arrived = last_sum(place, own, own_embed, received)
    slide_embed = jnp.transpose(arrived.reshape(capacity, lane_count, width), (1, 0, 2))
    return slide_embed[None, None], up_part, down_part


def solution(mesh):
    in_specs = (
        P("slide", "enc", None, None, None),
        P("slide", "enc", None),
        P("slide", None),
        P("slide", "enc", None, None, None),
        P(),
        P(),
        P(),
    )
    out_specs = (
        P("slide", "enc", None, None, None),
        P(("slide", "enc"), None),
        P(("slide", "enc"), None),
    )
    return jax.shard_map(body, mesh=mesh, in_specs=in_specs, out_specs=out_specs, check_vma=False)
```

```python
import functools

import jax
import jax.numpy as jnp
from jax import lax
from jax.experimental import pallas as pl
from jax.experimental.pallas import tpu as pltpu
from jax.sharding import PartitionSpec as P

root_half = 0.7071067811865476
half_log2_e = -0.7213475204444817
log2_inv_root_two_pi = -1.3257480647361592
axes = ("slide", "enc")
hops = (2, 1, 3)
VMEM = pl.BlockSpec(memory_space=pltpu.VMEM)
SMEM = pl.BlockSpec(memory_space=pltpu.SMEM)
HBM = pl.BlockSpec(memory_space=pltpu.HBM)
small_cost = pl.CostEstimate(flops=1000, bytes_accessed=1000, transcendentals=0)
nt = (((1,), (1,)), ((), ()))
tn = (((0,), (0,)), ((), ()))


def f32_dot(lhs, rhs, dims=(((1,), (0,)), ((), ()))):
    return lax.dot_general(lhs, rhs, dims, preferred_element_type=jnp.float32)


def row_hits(index, size):
    return index == lax.broadcasted_iota(jnp.int32, (index.shape[0], size), 1)


def slot_tables(counts_ref, owners_ref, table_ref, send_ref, place_ref):
    enc = lax.axis_index("enc")
    count, y, z = counts_ref[0, enc], enc // 4, enc % 4
    lanes, tiles = counts_ref.shape[1], owners_ref.shape[1]
    slot = lax.broadcasted_iota(jnp.int32, (tiles, tiles), 0)
    other = lax.broadcasted_iota(jnp.int32, (tiles, tiles), 1)
    line = jnp.broadcast_to(owners_ref[...], (tiles, tiles)).astype(jnp.float32)
    owners = jnp.sum(jnp.where(slot == other, line, 0.0), axis=1, keepdims=True)
    same = jnp.where((owners == line) & (other < slot), 1.0, 0.0)
    owners = owners.astype(jnp.int32)
    rank = jnp.sum(same, axis=1, keepdims=True).astype(jnp.int32)
    live = lax.broadcasted_iota(jnp.int32, (tiles, 1), 0) < count
    pick = lambda index, size, on: jnp.where(row_hits(index, size) & on, 1.0, 0.0).astype(jnp.bfloat16)
    table_ref[...] = pick(rank * lanes + owners, table_ref.shape[1], live)
    hops_y, hops_z = ((owners >> 2) - y) & 3, ((owners & 3) - z) & 3
    send_ref[...] = pick(hops_y * 16 + hops_z * 3 + rank, send_ref.shape[1], live)
    spots = lax.broadcasted_iota(jnp.int32, (place_ref.shape[0], 1), 0)
    reader = spots & (lanes - 1)
    from_y, from_z = (y - (reader >> 2)) & 3, (z - (reader & 3)) & 3
    place_ref[...] = pick(from_z * 16 + from_y * 3 + (spots >> 4), place_ref.shape[1], spots >= 0)


def conv_kernel(counts_ref, owners_ref, x_hbm, k_hbm, up_hbm, down_hbm, *rest):
    normed_ref, mean_ref, table_ref, send_ref, place_ref = rest[0:5]
    weights = rest[5:13]
    xb, kb, xf, kf, cv, sems = rest[13:]
    side = kb.shape[0]
    tiles, width = mean_ref.shape
    cells, reach = side * side, side // 2
    units = weights[0].shape[0]
    sub = units // 4
    slide, enc = lax.axis_index("slide"), lax.axis_index("enc")
    x, core, y = slide // 2, slide % 2, enc // 4
    first = jnp.where(core == 0, x, y)
    second = jnp.where(core == 0, y, x)

    def maps_copy(group):
        rows = pl.ds(group * 16, 16)
        return pltpu.make_async_copy(x_hbm.at[:, :, rows, :], xb.at[group], sems.at[group])

    def weight_copy(n):
        goal = lax.rem(first + (hops + (0,))[n % 16 // 4], 4)
        inner = lax.rem(second + n % 4 + 1, 4)
        row = jnp.where(core == 0, 8 * goal + inner, 8 * inner + goal) + 4 * core
        start = pl.ds(pl.multiple_of(row * sub, sub), sub)
        source = (up_hbm if n < 16 else down_hbm).at[start, :]
        goal = weights[n // 4].at[pl.ds(n % 4 * sub, sub), :]
        return pltpu.make_async_copy(source, goal, sems.at[3 + n])

    kernel_copy = pltpu.make_async_copy(k_hbm, kb, sems.at[2])
    kernel_copy.start()
    for group in range(tiles // 16):
        maps_copy(group).start()
    for n in range(32):
        weight_copy(n).start()
    slot_tables(counts_ref, owners_ref, table_ref, send_ref, place_ref)
    kernel_copy.wait()
    for n in range(cells):
        kf[n] = jnp.broadcast_to(
            kb[n // side, n % side : n % side + 1].astype(jnp.float32), (8, width)
        )

    @pl.loop(0, tiles // 16)
    def _(group):
        row = pl.multiple_of(group * 16, 16)
        maps_copy(group).wait()
        for n in range(cells):
            xf[n] = xb[group, n // side, n % side].astype(jnp.float32)

        @pl.loop(0, 2 * (width // 128))
        def _(unit):
            lane = pl.multiple_of((unit // 2) * 128, 128)
            half = pl.multiple_of((unit % 2) * 8, 8)
            for i in range(side):
                acc = [None] * side
                for a in range(side):
                    r = i + a - reach
                    if not 0 <= r < side:
                        continue
                    xs = [xf[r * side + j, pl.ds(half, 8), pl.ds(lane, 128)] for j in range(side)]
                    ks = [kf[a * side + b, :, pl.ds(lane, 128)] for b in range(side)]
                    for j in range(side):
                        for b in range(side):
                            c = j + b - reach
                            if 0 <= c < side:
                                term = xs[c] * ks[b]
                                acc[j] = term if acc[j] is None else acc[j] + term
                for j in range(side):
                    cv[i * side + j, pl.ds(half, 8), pl.ds(lane, 128)] = acc[j]

        total = None
        for n in range(cells):
            conv = cv[n]
            centred = conv - jnp.sum(conv, axis=1, keepdims=True) * (1.0 / width)
            var = jnp.sum(centred * centred, axis=1, keepdims=True) * (1.0 / width)
            normed_ref[n, pl.ds(row, 16), :] = (centred * lax.rsqrt(var + 1e-6)).astype(jnp.bfloat16)
            total = xf[n] if total is None else total + xf[n]
        mean_ref[pl.ds(row, 16), :] = total * (1.0 / cells)

    for n in range(32):
        weight_copy(n).wait()


def conv_norm(counts, owners, maps, kernel, up_weight, down_weight, capacity):
    side, _, tiles, width = maps.shape
    cells = side * side
    units = up_weight.shape[0] // 8
    shape = jax.ShapeDtypeStruct
    return pl.pallas_call(
        conv_kernel,
        out_shape=(
            shape((cells, tiles, width), jnp.bfloat16),
            shape((tiles, width), jnp.float32),
            shape((tiles, 16 * capacity), jnp.bfloat16),
            shape((tiles, 64), jnp.bfloat16),
            shape((16 * capacity, 64), jnp.bfloat16),
            *[shape((units, width), jnp.bfloat16)] * 8,
        ),
        in_specs=[SMEM, VMEM] + [HBM] * 4,
        out_specs=(VMEM,) * 13,
        scratch_shapes=[
            pltpu.VMEM((tiles // 16, side, side, 16, width), jnp.bfloat16),
            pltpu.VMEM(kernel.shape, jnp.bfloat16),
            pltpu.VMEM((cells, 16, width), jnp.float32),
            pltpu.VMEM((cells, 8, width), jnp.float32),
            pltpu.VMEM((cells, 16, width), jnp.float32),
            pltpu.SemaphoreType.DMA((35,)),
        ],
        compiler_params=pltpu.CompilerParams(vmem_limit_bytes=46 << 20),
        cost_estimate=small_cost,
        name="conv_norm",
    )(counts, owners.reshape(1, tiles), maps, kernel, up_weight, down_weight)


def gelu_pair(pre):
    cdf = 0.5 + 0.5 * lax.erf(pre * root_half)
    density = jnp.exp2(pre * pre * half_log2_e + log2_inv_root_two_pi)
    return pre * cdf, cdf + pre * density


def block_kernel(*rest):
    parts, sgs = rest[0:2], rest[2:4]
    up_s, dn_s, emb_ref, pay_ref, emb_out, grads = rest[4:]
    units = up_s.shape[0]
    tiles = sgs[0].shape[0]
    scale = 1.0 / (parts[0].shape[0] // tiles)
    up = up_s[...]
    both = jnp.concatenate([sg[...] for sg in sgs for _ in range(128 // tiles)], axis=0)
    dh_both = f32_dot(dn_s[...], both, nt) * scale
    dh = [dh_both[:, 0:128], dh_both[:, 128:256]]

    runs, tails = [], []
    for p, ref in enumerate(parts):
        full = ref.shape[0] // 256 * 256
        runs.append((p, full))
        for cut in range(full, ref.shape[0], 128):
            tails.append((p, cut, min(128, ref.shape[0] - cut)))
    tails.sort(key=lambda t: -t[2])
    pool = [jnp.zeros((units, 128), jnp.float32) for _ in range(2)]
    column = 0

    def tile(rhs, owners, column):
        pre = f32_dot(up, rhs, nt)
        at = 0
        for who, w in owners:
            hid, slope = gelu_pair(pre[:, at : at + w])
            grads[:, column + at : column + at + w] = (slope * dh[who][:, 0:w]).astype(jnp.bfloat16)
            if w < 128:
                hid = jnp.concatenate([hid, jnp.zeros((units, 128 - w), jnp.float32)], axis=1)
            pool[who] = pool[who] + hid
            at += w

    up_rows, waiting = None, None

    def absorb(todo, up_rows):
        start, size, rhs = todo
        term = f32_dot(grads[:, start : start + size], rhs())
        return term if up_rows is None else up_rows + term

    for p, full in runs:
        start = column
        for cut in range(0, full, 256):
            tile(parts[p][cut : cut + 256, :], [(p, 128)] * 2, column)
            column += 256
        if waiting is not None:
            up_rows = absorb(waiting, up_rows)
        waiting = (start, full, lambda p=p, full=full: parts[p][0:full, :])
    start = column
    group, size = [], 0
    for n, (p, cut, w) in enumerate(tails):
        group.append((p, cut, w))
        size += w
        if size == 256 or n == len(tails) - 1:
            rhs = jnp.concatenate([parts[q][c : c + v, :] for q, c, v in group], axis=0)
            tile(rhs, [(q, v) for q, _, v in group], column)
            column += size
            group, size = [], 0
    up_rows = absorb(waiting, up_rows)
    rhs = jnp.concatenate([parts[p][c : c + w, :] for p, c, w in tails], axis=0)
    up_rows = absorb((start, column - start, lambda: rhs), up_rows)
    pay_ref[0:units] = up_rows.astype(jnp.bfloat16)

    pick = (
        lax.broadcasted_iota(jnp.int32, (tiles, 128), 0)
        == lax.broadcasted_iota(jnp.int32, (tiles, 128), 1)
    ).astype(jnp.bfloat16)
    flat = []
    for value in pool:
        shift = 64
        while shift >= tiles:
            value = value + pltpu.roll(value, shift, 1)
            shift //= 2
        flat.append(f32_dot(pick, (value * scale).astype(jnp.bfloat16), nt).astype(jnp.bfloat16))
    emb_out[...] = emb_ref[...] + f32_dot(jnp.concatenate(flat, axis=0), dn_s[...])
    for h in range(2):
        pay_ref[units + h * tiles : units + (h + 1) * tiles] = sgs[h][...]
        pay_ref[units + 2 * tiles : units + 3 * tiles, h * units : (h + 1) * units] = flat[h]


def hidden_block(parts, grads, up, down, emb):
    tiles, width = grads[0].shape
    units = up.shape[0]
    rows = sum(p.shape[0] for p in parts)
    return pl.pallas_call(
        block_kernel,
        out_shape=(
            jax.ShapeDtypeStruct((units + 3 * tiles, width), jnp.bfloat16),
            jax.ShapeDtypeStruct((2 * tiles, width), jnp.float32),
        ),
        in_specs=[VMEM] * 7,
        out_specs=(VMEM, VMEM),
        scratch_shapes=[pltpu.VMEM((units, rows), jnp.bfloat16)],
        compiler_params=pltpu.CompilerParams(vmem_limit_bytes=16 << 20),
        cost_estimate=small_cost,
        name="hidden_block",
    )(*parts, *grads, up, down, emb)


def combine_kernel(a_ref, b_ref, c_ref, d_ref, *outs):
    units = outs[0].shape[0] * 4
    width = a_ref.shape[1]
    tiles = (a_ref.shape[0] - units) // 3
    refs = (a_ref, b_ref, c_ref, d_ref)
    up = None
    for r in refs:
        term = r[0:units].astype(jnp.float32)
        up = term if up is None else up + term
    sg = jnp.concatenate([r[units : units + 2 * tiles] for r in refs], axis=0)
    low, high = units + 2 * tiles, units + 3 * tiles
    pool = jnp.concatenate(
        [r[low:high, h * units : (h + 1) * units] for r in refs for h in range(2)], axis=0
    )
    down = f32_dot(pool, sg, tn)
    sub = units // 4
    for q, out in enumerate(outs):
        out[:, 0:width] = up[q * sub : (q + 1) * sub].astype(out.dtype)
        out[:, width : 2 * width] = down[q * sub : (q + 1) * sub].astype(out.dtype)


def combine(payloads, units):
    width = payloads[0].shape[1]
    shape = lambda dtype: jax.ShapeDtypeStruct((units // 4, 2 * width), dtype)
    return pl.pallas_call(
        combine_kernel,
        out_shape=(shape(jnp.bfloat16),) * 3 + (shape(jnp.float32),),
        in_specs=[VMEM] * 4,
        out_specs=(VMEM,) * 4,
        compiler_params=pltpu.CompilerParams(vmem_limit_bytes=16 << 20),
        cost_estimate=small_cost,
        name="combine",
    )(*payloads)


def embed_kernel(table_ref, mean_ref, emb_ref, other_ref, *outs):
    tiles = mean_ref.shape[0]
    embed = (mean_ref[...] + emb_ref[0:tiles] + other_ref[...]).astype(jnp.bfloat16)
    sorted_rows = f32_dot(table_ref[...], embed, tn).astype(jnp.bfloat16)
    for k, out in enumerate(outs):
        out[...] = sorted_rows[16 * k : 16 * k + 16]


def embed_rows(table, mean, emb, other):
    width = mean.shape[1]
    return pl.pallas_call(
        embed_kernel,
        out_shape=(jax.ShapeDtypeStruct((16, width), jnp.bfloat16),) * 4,
        in_specs=[VMEM] * 4,
        out_specs=(VMEM,) * 4,
        compiler_params=pltpu.CompilerParams(vmem_limit_bytes=4 << 20),
        cost_estimate=small_cost,
        name="embed_rows",
    )(table, mean, emb, other)


def second_kernel(own_ref, *rest):
    z = lax.axis_index("enc") % 4
    received, embeds = rest[0:3], rest[3:7]
    own_out, pays, embed_out, total = rest[7], rest[8:11], rest[11], rest[12]
    width = own_out.shape[1]
    last = own_ref.shape[0] // 4
    total[...] = own_ref[...] + sum(r[...].astype(jnp.float32) for r in received)
    row = lax.broadcasted_iota(jnp.int32, (64, 64), 0)
    col = lax.broadcasted_iota(jnp.int32, (64, 64), 1)
    match = None
    for j in range(4):
        for k in range(4):
            rank = row - (16 * j + 3 * k)
            hit = (rank >= 0) & (rank < 3) & (col == 16 * k + 3 * j + rank)
            match = hit if match is None else match | hit
    embeds = jnp.concatenate([e[...] for e in embeds], axis=0)
    embeds = f32_dot(match.astype(jnp.bfloat16), embeds)
    for j in range(4):
        rows = pl.ds(pl.multiple_of(lax.rem(z + j, 4) * last, 8), last)
        up, down = total[rows, 0:width], total[rows, width : 2 * width]
        if j == 0:
            own_out[...] = jnp.concatenate([up, down], axis=0)
            embed_out[...] = embeds[0:16].astype(jnp.bfloat16)
        else:
            pays[j - 1][...] = jnp.concatenate(
                [up, down, embeds[16 * j : 16 * j + 16]], axis=0
            ).astype(jnp.bfloat16)


def second_sum(own, received, embeds):
    sub, width = own.shape[0], own.shape[1] // 2
    rows = sub // 2
    return pl.pallas_call(
        second_kernel,
        out_shape=(
            jax.ShapeDtypeStruct((rows, width), jnp.float32),
            *[jax.ShapeDtypeStruct((rows + 16, width), jnp.bfloat16)] * 3,
            jax.ShapeDtypeStruct((16, width), jnp.bfloat16),
        ),
        in_specs=[VMEM] * 8,
        out_specs=(VMEM,) * 5,
        scratch_shapes=[pltpu.VMEM(own.shape, jnp.float32)],
        compiler_params=pltpu.CompilerParams(vmem_limit_bytes=8 << 20),
        cost_estimate=small_cost,
        name="second_sum",
    )(own, *received, *embeds)


def last_kernel(place_ref, own_ref, embed_ref, a_ref, b_ref, c_ref, up_ref, down_ref, out_ref):
    half = up_ref.shape[0]
    rows = 2 * half
    total = own_ref[...]
    for r in (a_ref, b_ref, c_ref):
        total = total + r[...].astype(jnp.float32)[0:rows]
    up_ref[...] = total[0:half]
    down_ref[...] = total[half:rows]
    embeds = jnp.concatenate(
        [embed_ref[...]] + [r[rows : rows + 16] for r in (a_ref, b_ref, c_ref)], axis=0
    )
    out_ref[...] = f32_dot(place_ref[...], embeds).astype(jnp.bfloat16)


def last_sum(place, own, embed, received):
    rows, width = own.shape
    return pl.pallas_call(
        last_kernel,
        out_shape=(
            jax.ShapeDtypeStruct((rows // 2, width), jnp.float32),
            jax.ShapeDtypeStruct((rows // 2, width), jnp.float32),
            jax.ShapeDtypeStruct((place.shape[0], width), jnp.bfloat16),
        ),
        in_specs=[VMEM] * 6,
        out_specs=(VMEM,) * 3,
        compiler_params=pltpu.CompilerParams(vmem_limit_bytes=4 << 20),
        cost_estimate=small_cost,
        name="last_sum",
    )(place, own, embed, *received)


def move(value, stage, hop):
    pairs = []
    for x in range(4):
        for c in range(2):
            for y in range(4):
                for z in range(4):
                    to = [x, c, y, z]
                    if stage == 0:
                        to[1] = 1 - c
                    else:
                        spot = {1: 2 * c, 2: 2 - 2 * c, 3: 3, 4: 2}[stage]
                        to[spot] = (to[spot] + hop) % 4
                    line = lambda p: (p[0] * 2 + p[1]) * 16 + p[2] * 4 + p[3]
                    pairs.append((line((x, c, y, z)), line(to)))
    return lax.ppermute(value, axes, pairs)


def body(tile_maps, tile_owner, tissue_counts, embed_grad, depth_kernel, up_weight, down_weight):
    lane_count = lax.axis_size("enc")
    maps = jnp.transpose(tile_maps[0], (1, 2, 0, 3))
    side, _, tiles, width = maps.shape
    units = up_weight.shape[0] // 8
    capacity = embed_grad.shape[3]

    fetched = lax.all_to_all(
        jnp.transpose(embed_grad[0, 0], (1, 0, 2)), "enc", split_axis=1, concat_axis=1, tiled=True
    )

    normed, map_mean, table, send_table, place, *weights = conv_norm(
        tissue_counts, tile_owner, maps, depth_kernel, up_weight, down_weight, capacity
    )
    normed = normed.reshape(-1, width)
    sib_normed = move(normed, 0, 0)

    slot_grad = f32_dot(table, fetched.reshape(capacity * lane_count, width)).astype(jnp.bfloat16)
    sib_grad = move(slot_grad, 0, 0)

    emb = jnp.zeros((2 * tiles, width), jnp.float32)
    payloads = []
    for n, hop in enumerate(hops + (0,)):
        if not hop:
            emb, payloads[0] = lax.optimization_barrier((emb, payloads[0]))
        pay, emb = hidden_block(
            (normed, sib_normed), (slot_grad, sib_grad), weights[n], weights[4 + n], emb
        )
        payloads.append(move(pay, 1, hop) if hop else pay)

    other_emb = move(emb[tiles:], 0, 0)
    payloads[1], other_emb = lax.optimization_barrier((payloads[1], other_emb))
    rows_out = embed_rows(send_table, map_mean, emb, other_emb)
    payloads, rows_out = lax.optimization_barrier((payloads, rows_out))

    parts = combine(payloads, units)
    received = [move(parts[hop - 1], 2, hop) for hop in hops]
    by_hop = {hop: move(rows_out[hop], 4, hop) for hop in hops}
    by_hop[0] = rows_out[0]
    own, *pays, own_embed = second_sum(parts[3], received, [by_hop[hop] for hop in range(4)])
    by_hop = {hop: move(pays[hop - 1], 3, hop) for hop in hops}
    up_part, down_part, arrived = last_sum(
        place, own, own_embed, [by_hop[hop] for hop in (1, 2, 3)]
    )
    slide_embed = jnp.transpose(arrived.reshape(capacity, lane_count, width), (1, 0, 2))
    return slide_embed[None, None], up_part, down_part


def solution(mesh):
    in_specs = (
        P("slide", "enc", None, None, None),
        P("slide", "enc", None),
        P("slide", None),
        P("slide", "enc", None, None, None),
        P(),
        P(),
        P(),
    )
    out_specs = (
        P("slide", "enc", None, None, None),
        P(("slide", "enc"), None),
        P(("slide", "enc"), None),
    )
    return jax.shard_map(body, mesh=mesh, in_specs=in_specs, out_specs=out_specs, check_vma=False)
```

```python
import functools

import jax
import jax.numpy as jnp
from jax import lax
from jax.experimental import pallas as pl
from jax.experimental.pallas import tpu as pltpu
from jax.sharding import PartitionSpec as P

root_half = 0.7071067811865476
half_log2_e = -0.7213475204444817
log2_inv_root_two_pi = -1.3257480647361592
axes = ("slide", "enc")
hops = (2, 1, 3)
VMEM = pl.BlockSpec(memory_space=pltpu.VMEM)
SMEM = pl.BlockSpec(memory_space=pltpu.SMEM)
HBM = pl.BlockSpec(memory_space=pltpu.HBM)
small_cost = pl.CostEstimate(flops=1000, bytes_accessed=1000, transcendentals=0)
large_cost = pl.CostEstimate(flops=20_000_000_000, bytes_accessed=1000, transcendentals=0)
nt = (((1,), (1,)), ((), ()))
tn = (((0,), (0,)), ((), ()))


def f32_dot(lhs, rhs, dims=(((1,), (0,)), ((), ()))):
    return lax.dot_general(lhs, rhs, dims, preferred_element_type=jnp.float32)


def row_hits(index, size):
    return index == lax.broadcasted_iota(jnp.int32, (index.shape[0], size), 1)


def slot_tables(counts_ref, owners_ref, table_ref, send_ref, place_ref):
    enc, core = lax.axis_index("enc"), lax.axis_index("slide") % 2
    count, y, z = counts_ref[0, enc], enc // 4, enc % 4
    lanes, tiles = counts_ref.shape[1], owners_ref.shape[1]
    slot = lax.broadcasted_iota(jnp.int32, (tiles, tiles), 0)
    other = lax.broadcasted_iota(jnp.int32, (tiles, tiles), 1)
    line = jnp.broadcast_to(owners_ref[...], (tiles, tiles)).astype(jnp.float32)
    owners = jnp.sum(jnp.where(slot == other, line, 0.0), axis=1, keepdims=True)
    same = jnp.where((owners == line) & (other < slot), 1.0, 0.0)
    owners = owners.astype(jnp.int32)
    rank = jnp.sum(same, axis=1, keepdims=True).astype(jnp.int32)
    live = lax.broadcasted_iota(jnp.int32, (tiles, 1), 0) < count
    pick = lambda index, size, on: jnp.where(row_hits(index, size) & on, 1.0, 0.0).astype(jnp.bfloat16)
    hops_y, hops_z = ((owners >> 2) - y) & 3, ((owners & 3) - z) & 3
    table_ref[...] = pick(((4 - hops_z) & 3) * 16 + ((4 - hops_y) & 3) * 3 + rank, 64, live)
    one, two = (hops_z, hops_y), (hops_y, hops_z)
    near, far = [jnp.where(core == 0, p, q) for p, q in zip(one, two)]
    send_ref[...] = pick(near * 16 + far * 3 + rank, 64, live)
    spots = lax.broadcasted_iota(jnp.int32, (place_ref.shape[0], 1), 0)
    reader = spots & (lanes - 1)
    from_y, from_z = (y - (reader >> 2)) & 3, (z - (reader & 3)) & 3
    near = jnp.where(core == 0, from_z, from_y)
    far = jnp.where(core == 0, from_y, from_z)
    place_ref[...] = pick(far * 16 + near * 3 + (spots >> 4), 64, spots >= 0)


def conv_kernel(counts_ref, owners_ref, x_hbm, k_hbm, up_hbm, down_hbm, *rest):
    normed_ref, mean_ref, table_ref, send_ref, place_ref = rest[0:5]
    weights = rest[5:13]
    xb, kb, xf, kf, cv, sems = rest[13:]
    side = kb.shape[0]
    tiles, width = mean_ref.shape
    cells, reach = side * side, side // 2
    units = weights[0].shape[0]
    sub = units // 4
    slide, enc = lax.axis_index("slide"), lax.axis_index("enc")
    x, core, y = slide // 2, slide % 2, enc // 4
    first = jnp.where(core == 0, x, y)

    def maps_copy(group):
        rows = pl.ds(group * 16, 16)
        return pltpu.make_async_copy(x_hbm.at[:, :, rows, :], xb.at[group], sems.at[group])

    def weight_copy(n):
        goal = lax.rem(first + (hops + (0,))[n % 16 // 4], 4)
        row = jnp.where(core == 0, 8 * goal + n % 4, 8 * (n % 4) + goal) + 4 * core
        start = pl.ds(pl.multiple_of(row * sub, sub), sub)
        source = (up_hbm if n < 16 else down_hbm).at[start, :]
        goal = weights[n // 4].at[pl.ds(n % 4 * sub, sub), :]
        return pltpu.make_async_copy(source, goal, sems.at[3 + n])

    kernel_copy = pltpu.make_async_copy(k_hbm, kb, sems.at[2])
    kernel_copy.start()
    for group in range(tiles // 16):
        maps_copy(group).start()
    slot_tables(counts_ref, owners_ref, table_ref, send_ref, place_ref)
    for n in range(32):
        weight_copy(n).start()
    kernel_copy.wait()
    for n in range(cells):
        kf[n] = jnp.broadcast_to(
            kb[n // side, n % side : n % side + 1].astype(jnp.float32), (8, width)
        )

    @pl.loop(0, tiles // 16)
    def _(group):
        row = pl.multiple_of(group * 16, 16)
        maps_copy(group).wait()
        for n in range(cells):
            xf[n] = xb[group, n // side, n % side].astype(jnp.float32)

        @pl.loop(0, 2 * (width // 128))
        def _(unit):
            lane = pl.multiple_of((unit // 2) * 128, 128)
            half = pl.multiple_of((unit % 2) * 8, 8)
            for i in range(side):
                acc = [None] * side
                for a in range(side):
                    r = i + a - reach
                    if not 0 <= r < side:
                        continue
                    xs = [xf[r * side + j, pl.ds(half, 8), pl.ds(lane, 128)] for j in range(side)]
                    ks = [kf[a * side + b, :, pl.ds(lane, 128)] for b in range(side)]
                    for j in range(side):
                        for b in range(side):
                            c = j + b - reach
                            if 0 <= c < side:
                                term = xs[c] * ks[b]
                                acc[j] = term if acc[j] is None else acc[j] + term
                for j in range(side):
                    cv[i * side + j, pl.ds(half, 8), pl.ds(lane, 128)] = acc[j]

        total = None
        for n in range(cells):
            conv = cv[n]
            centred = conv - jnp.sum(conv, axis=1, keepdims=True) * (1.0 / width)
            var = jnp.sum(centred * centred, axis=1, keepdims=True) * (1.0 / width)
            normed_ref[n, pl.ds(row, 16), :] = (centred * lax.rsqrt(var + 1e-6)).astype(jnp.bfloat16)
            total = xf[n] if total is None else total + xf[n]
        mean_ref[pl.ds(row, 16), :] = total * (1.0 / cells)

    for n in range(32):
        weight_copy(n).wait()


def conv_norm(counts, owners, maps, kernel, up_weight, down_weight, capacity):
    side, _, tiles, width = maps.shape
    cells = side * side
    units = up_weight.shape[0] // 8
    shape = jax.ShapeDtypeStruct
    return pl.pallas_call(
        conv_kernel,
        out_shape=(
            shape((cells, tiles, width), jnp.bfloat16),
            shape((tiles, width), jnp.float32),
            shape((tiles, 64), jnp.bfloat16),
            shape((tiles, 64), jnp.bfloat16),
            shape((16 * capacity, 64), jnp.bfloat16),
            *[shape((units, width), jnp.bfloat16)] * 8,
        ),
        in_specs=[SMEM, VMEM] + [HBM] * 4,
        out_specs=(VMEM,) * 13,
        scratch_shapes=[
            pltpu.VMEM((tiles // 16, side, side, 16, width), jnp.bfloat16),
            pltpu.VMEM(kernel.shape, jnp.bfloat16),
            pltpu.VMEM((cells, 16, width), jnp.float32),
            pltpu.VMEM((cells, 8, width), jnp.float32),
            pltpu.VMEM((cells, 16, width), jnp.float32),
            pltpu.SemaphoreType.DMA((35,)),
        ],
        compiler_params=pltpu.CompilerParams(vmem_limit_bytes=46 << 20),
        cost_estimate=small_cost,
        name="conv_norm",
    )(counts, owners.reshape(1, tiles), maps, kernel, up_weight, down_weight)


def gelu_pair(pre):
    cdf = 0.5 + 0.5 * lax.erf(pre * root_half)
    density = jnp.exp2(pre * pre * half_log2_e + log2_inv_root_two_pi)
    return pre * cdf, cdf + pre * density


def block_kernel(*rest):
    parts, sgs = rest[0:2], rest[2:4]
    up_s, dn_s, emb_ref, pay_ref, emb_out, grads = rest[4:]
    units = up_s.shape[0]
    tiles = sgs[0].shape[0]
    scale = 1.0 / (parts[0].shape[0] // tiles)
    up = up_s[...]
    both = jnp.concatenate([sg[...] for sg in sgs for _ in range(128 // tiles)], axis=0)
    dh_both = f32_dot(dn_s[...], both, nt) * scale
    dh = [dh_both[:, 0:128], dh_both[:, 128:256]]

    runs, tails = [], []
    for p, ref in enumerate(parts):
        full = ref.shape[0] // 256 * 256
        runs.append((p, full))
        for cut in range(full, ref.shape[0], 128):
            tails.append((p, cut, min(128, ref.shape[0] - cut)))
    tails.sort(key=lambda t: -t[2])
    pool = [jnp.zeros((units, 128), jnp.float32) for _ in range(2)]
    column = 0

    def tile(rhs, owners, column):
        pre = f32_dot(up, rhs, nt)
        at = 0
        for who, w in owners:
            hid, slope = gelu_pair(pre[:, at : at + w])
            grads[:, column + at : column + at + w] = (slope * dh[who][:, 0:w]).astype(jnp.bfloat16)
            if w < 128:
                hid = jnp.concatenate([hid, jnp.zeros((units, 128 - w), jnp.float32)], axis=1)
            pool[who] = pool[who] + hid
            at += w

    up_rows, waiting = None, None

    def absorb(todo, up_rows):
        start, size, rhs = todo
        term = f32_dot(grads[:, start : start + size], rhs())
        return term if up_rows is None else up_rows + term

    for p, full in runs:
        start = column
        for cut in range(0, full, 256):
            tile(parts[p][cut : cut + 256, :], [(p, 128)] * 2, column)
            column += 256
        if waiting is not None:
            up_rows = absorb(waiting, up_rows)
        waiting = (start, full, lambda p=p, full=full: parts[p][0:full, :])
    start = column
    group, size = [], 0
    for n, (p, cut, w) in enumerate(tails):
        group.append((p, cut, w))
        size += w
        if size == 256 or n == len(tails) - 1:
            rhs = jnp.concatenate([parts[q][c : c + v, :] for q, c, v in group], axis=0)
            tile(rhs, [(q, v) for q, _, v in group], column)
            column += size
            group, size = [], 0
    up_rows = absorb(waiting, up_rows)
    rhs = jnp.concatenate([parts[p][c : c + w, :] for p, c, w in tails], axis=0)
    up_rows = absorb((start, column - start, lambda: rhs), up_rows)
    pay_ref[0:units] = up_rows.astype(jnp.bfloat16)

    pick = (
        lax.broadcasted_iota(jnp.int32, (tiles, 128), 0)
        == lax.broadcasted_iota(jnp.int32, (tiles, 128), 1)
    ).astype(jnp.bfloat16)
    flat = []
    for value in pool:
        shift = 64
        while shift >= tiles:
            value = value + pltpu.roll(value, shift, 1)
            shift //= 2
        flat.append(f32_dot(pick, (value * scale).astype(jnp.bfloat16), nt).astype(jnp.bfloat16))
    emb_out[...] = emb_ref[...] + f32_dot(jnp.concatenate(flat, axis=0), dn_s[...])
    for h in range(2):
        pay_ref[units + h * tiles : units + (h + 1) * tiles] = sgs[h][...]
        pay_ref[units + 2 * tiles : units + 3 * tiles, h * units : (h + 1) * units] = flat[h]


def hidden_block(parts, grads, up, down, emb):
    tiles, width = grads[0].shape
    units = up.shape[0]
    rows = sum(p.shape[0] for p in parts)
    return pl.pallas_call(
        block_kernel,
        out_shape=(
            jax.ShapeDtypeStruct((units + 3 * tiles, width), jnp.bfloat16),
            jax.ShapeDtypeStruct((2 * tiles, width), jnp.float32),
        ),
        in_specs=[VMEM] * 7,
        out_specs=(VMEM, VMEM),
        scratch_shapes=[pltpu.VMEM((units, rows), jnp.bfloat16)],
        compiler_params=pltpu.CompilerParams(vmem_limit_bytes=16 << 20),
        cost_estimate=small_cost,
        name="hidden_block",
    )(*parts, *grads, up, down, emb)


def one_hot_rows(target, rows):
    hit = lax.broadcasted_iota(jnp.int32, (rows, target.shape[1]), 0) == target
    return jnp.where(hit, 1.0, 0.0).astype(jnp.bfloat16)


def regroup(blocks):
    col = lax.broadcasted_iota(jnp.int32, (1, 64), 1)
    spot = col & 15
    far = jnp.where(spot < 3, 0, jnp.where(spot < 6, 1, jnp.where(spot < 9, 2, 3)))
    target = jnp.where(spot < 12, 16 * far + 3 * (col >> 4) + spot - 3 * far, -1)
    return f32_dot(one_hot_rows(target, 64), jnp.concatenate(blocks, axis=0))


def spread_kernel(grad_ref, *outs):
    enc = lax.axis_index("enc")
    y, z = enc // 4, enc % 4
    col = lax.broadcasted_iota(jnp.int32, (1, grad_ref.shape[0]), 1)
    reader = col & 15
    target = (((reader >> 2) - y) & 3) * 16 + (((reader & 3) - z) & 3) * 3 + (col >> 4)
    rows = f32_dot(one_hot_rows(target, 64), grad_ref[...]).astype(jnp.bfloat16)
    for k, out in enumerate(outs):
        out[...] = rows[16 * k : 16 * k + 16]


def regroup_kernel(*refs):
    rows = regroup([r[...] for r in refs[0:4]]).astype(jnp.bfloat16)
    for k, out in enumerate(refs[4:]):
        out[...] = rows[16 * k : 16 * k + 16]


def slot_kernel(table_ref, *refs):
    rows = jnp.concatenate([r[...] for r in refs[0:4]], axis=0)
    refs[4][...] = f32_dot(table_ref[...], rows).astype(jnp.bfloat16)


def small_call(kernel, name, args, shapes, cost):
    return pl.pallas_call(
        kernel,
        out_shape=tuple(jax.ShapeDtypeStruct(dims, jnp.bfloat16) for dims in shapes),
        in_specs=[VMEM] * len(args),
        out_specs=(VMEM,) * len(shapes),
        compiler_params=pltpu.CompilerParams(vmem_limit_bytes=4 << 20),
        cost_estimate=cost,
        name=name,
    )(*args)


def spread_rows(grads):
    return small_call(spread_kernel, "spread_rows", (grads,), [(16, grads.shape[1])] * 4, small_cost)


def regroup_rows(blocks):
    return small_call(regroup_kernel, "regroup_rows", blocks, [blocks[0].shape] * 4, large_cost)


def slot_rows(table, blocks):
    dims = (table.shape[0], blocks[0].shape[1])
    return small_call(slot_kernel, "slot_rows", (table, *blocks), [dims], large_cost)[0]


def combine_kernel(a_ref, b_ref, c_ref, d_ref, table_ref, mean_ref, emb_ref, other_ref, *outs):
    pays, own_out, embeds, total = outs[0:3], outs[3], outs[4:8], outs[8]
    slide, enc = lax.axis_index("slide"), lax.axis_index("enc")
    x, core, z = slide // 2, slide % 2, enc % 4
    units = total.shape[0]
    width = a_ref.shape[1]
    tiles = (a_ref.shape[0] - units) // 3
    refs = (a_ref, b_ref, c_ref, d_ref)
    embed = (mean_ref[...] + emb_ref[0:tiles] + other_ref[...]).astype(jnp.bfloat16)
    rows = f32_dot(table_ref[...], embed, tn)
    up = None
    for r in refs:
        term = r[0:units].astype(jnp.float32)
        up = term if up is None else up + term
    sg = jnp.concatenate([r[units : units + 2 * tiles] for r in refs], axis=0)
    low, high = units + 2 * tiles, units + 3 * tiles
    pool = jnp.concatenate(
        [r[low:high, h * units : (h + 1) * units] for r in refs for h in range(2)], axis=0
    )
    total[:, 0:width] = up
    total[:, width : 2 * width] = f32_dot(pool, sg, tn)
    sub, last = units // 4, units // 16
    for hop in range(4):
        pieces = []
        for i in range(4):
            on_z = i * sub + ((z + hop) & 3) * last
            on_x = ((x + hop) & 3) * sub + i * last
            start = pl.multiple_of(jnp.where(core == 0, on_z, on_x), 8)
            pieces.append(total[pl.ds(start, last), :])
        mine = rows[16 * hop : 16 * hop + 16]
        embeds[hop][...] = mine.astype(jnp.bfloat16)
        if hop:
            pieces.append(jnp.concatenate([mine[0:8], mine[8:16]], axis=1))
            pays[hop - 1][...] = jnp.concatenate(pieces, axis=0).astype(jnp.bfloat16)
        else:
            own_out[...] = jnp.concatenate(pieces, axis=0)


def combine(payloads, units, table, mean, emb, other):
    width = payloads[0].shape[1]
    shape = jax.ShapeDtypeStruct
    return pl.pallas_call(
        combine_kernel,
        out_shape=(
            *[shape((units // 4 + 8, 2 * width), jnp.bfloat16)] * 3,
            shape((units // 4, 2 * width), jnp.float32),
            *[shape((16, width), jnp.bfloat16)] * 4,
        ),
        in_specs=[VMEM] * 8,
        out_specs=(VMEM,) * 8,
        scratch_shapes=[pltpu.VMEM((units, 2 * width), jnp.float32)],
        compiler_params=pltpu.CompilerParams(vmem_limit_bytes=16 << 20),
        cost_estimate=small_cost,
        name="combine",
    )(*payloads, table, mean, emb, other)


def second_kernel(own_ref, *rest):
    received, own_embed, moved = rest[0:3], rest[3], rest[4:7]
    own_out, pays, embed_out, total = rest[7], rest[8:11], rest[11], rest[12]
    core, enc = lax.axis_index("slide") % 2, lax.axis_index("enc")
    third = jnp.where(core == 0, enc // 4, enc % 4)
    width = own_out.shape[1]
    sub = own_ref.shape[0]
    last = sub // 4
    received = [r[...].astype(jnp.float32) for r in received]
    total[...] = own_ref[...] + sum(r[0:sub] for r in received)
    blocks = [own_embed[...]]
    for r, other in zip(received, moved):
        ridden = jnp.concatenate([r[sub:, 0:width], r[sub:, width : 2 * width]], axis=0)
        block = jnp.where(core == 0, ridden, other[...].astype(jnp.float32))
        blocks.append(block.astype(jnp.bfloat16))
    embeds = regroup(blocks)
    for hop in range(4):
        rows = pl.ds(pl.multiple_of(((third + hop) & 3) * last, 8), last)
        up, down = total[rows, 0:width], total[rows, width : 2 * width]
        if hop == 0:
            own_out[...] = jnp.concatenate([up, down], axis=0)
            embed_out[...] = embeds[0:16].astype(jnp.bfloat16)
        else:
            pays[hop - 1][...] = jnp.concatenate(
                [up, down, embeds[16 * hop : 16 * hop + 16]], axis=0
            ).astype(jnp.bfloat16)


def second_sum(own, received, own_embed, moved):
    sub, width = own.shape[0], own.shape[1] // 2
    rows = sub // 2
    return pl.pallas_call(
        second_kernel,
        out_shape=(
            jax.ShapeDtypeStruct((rows, width), jnp.float32),
            *[jax.ShapeDtypeStruct((rows + 16, width), jnp.bfloat16)] * 3,
            jax.ShapeDtypeStruct((16, width), jnp.bfloat16),
        ),
        in_specs=[VMEM] * 8,
        out_specs=(VMEM,) * 5,
        scratch_shapes=[pltpu.VMEM(own.shape, jnp.float32)],
        compiler_params=pltpu.CompilerParams(vmem_limit_bytes=8 << 20),
        cost_estimate=small_cost,
        name="second_sum",
    )(own, *received, own_embed, *moved)


def last_kernel(place_ref, own_ref, embed_ref, a_ref, b_ref, c_ref, up_ref, down_ref, out_ref):
    half = up_ref.shape[0]
    rows = 2 * half
    total = own_ref[...]
    for r in (a_ref, b_ref, c_ref):
        total = total + r[...].astype(jnp.float32)[0:rows]
    up_ref[...] = total[0:half]
    down_ref[...] = total[half:rows]
    embeds = jnp.concatenate(
        [embed_ref[...]] + [r[rows : rows + 16] for r in (a_ref, b_ref, c_ref)], axis=0
    )
    out_ref[...] = f32_dot(place_ref[...], embeds).astype(jnp.bfloat16)


def last_sum(place, own, embed, received):
    rows, width = own.shape
    return pl.pallas_call(
        last_kernel,
        out_shape=(
            jax.ShapeDtypeStruct((rows // 2, width), jnp.float32),
            jax.ShapeDtypeStruct((rows // 2, width), jnp.float32),
            jax.ShapeDtypeStruct((place.shape[0], width), jnp.bfloat16),
        ),
        in_specs=[VMEM] * 6,
        out_specs=(VMEM,) * 3,
        compiler_params=pltpu.CompilerParams(vmem_limit_bytes=4 << 20),
        cost_estimate=small_cost,
        name="last_sum",
    )(place, own, embed, *received)


def move(value, stage, hop):
    spots = {0: (1, 1), 1: (0, 2), 2: (3, 0), 3: (2, 3), 4: (2, 2), 5: (3, 3)}[stage]
    pairs = []
    for x in range(4):
        for core in range(2):
            for y in range(4):
                for z in range(4):
                    here, there = [x, core, y, z], [x, core, y, z]
                    if stage == 0:
                        there[1] = 1 - core
                    else:
                        there[spots[core]] = (there[spots[core]] + hop) % 4
                    line = lambda p: (p[0] * 2 + p[1]) * 16 + p[2] * 4 + p[3]
                    pairs.append((line(here), line(there)))
    return lax.ppermute(value, axes, pairs)


def body(tile_maps, tile_owner, tissue_counts, embed_grad, depth_kernel, up_weight, down_weight):
    lane_count = lax.axis_size("enc")
    maps = jnp.transpose(tile_maps[0], (1, 2, 0, 3))
    side, _, tiles, width = maps.shape
    units = up_weight.shape[0] // 8
    capacity = embed_grad.shape[3]

    sent = spread_rows(jnp.transpose(embed_grad[0, 0], (1, 0, 2)).reshape(-1, width))
    arrived = [move(sent[hop], 4, hop) for hop in (1, 2, 3)]
    tissue_counts, sent = lax.optimization_barrier((tissue_counts, sent))
    normed, map_mean, table, send_table, place, *weights = conv_norm(
        tissue_counts, tile_owner, maps, depth_kernel, up_weight, down_weight, capacity
    )
    normed = normed.reshape(-1, width)
    sib_normed = move(normed, 0, 0)
    table, arrived = lax.optimization_barrier((table, arrived))
    sent = regroup_rows((sent[0], *arrived))
    arrived = [move(sent[hop], 5, hop) for hop in (1, 2, 3)]
    slot_grad = slot_rows(table, (sent[0], *arrived))
    sib_grad = move(slot_grad, 0, 0)

    emb = jnp.zeros((2 * tiles, width), jnp.float32)
    payloads = []
    for n, hop in enumerate(hops + (0,)):
        if not hop:
            emb, payloads[0] = lax.optimization_barrier((emb, payloads[0]))
        pay, emb = hidden_block(
            (normed, sib_normed), (slot_grad, sib_grad), weights[n], weights[4 + n], emb
        )
        payloads.append(move(pay, 1, hop) if hop else pay)

    other_emb = move(emb[tiles:], 0, 0)
    payloads[1], other_emb = lax.optimization_barrier((payloads[1], other_emb))
    *pays, own, own_embed, embed_1, embed_2, embed_3 = combine(
        payloads, units, send_table, map_mean, emb, other_emb
    )
    received = [move(pays[hop - 1], 2, hop) for hop in (1, 2, 3)]
    moved = [move(rows, 4, hop) for hop, rows in ((1, embed_1), (2, embed_2), (3, embed_3))]
    own, *pays, own_embed = second_sum(own, received, own_embed, moved)
    by_hop = {hop: move(pays[hop - 1], 3, hop) for hop in (1, 2, 3)}
    up_part, down_part, arrived = last_sum(
        place, own, own_embed, [by_hop[hop] for hop in (1, 2, 3)]
    )
    slide_embed = jnp.transpose(arrived.reshape(capacity, lane_count, width), (1, 0, 2))
    return slide_embed[None, None], up_part, down_part


def solution(mesh):
    in_specs = (
        P("slide", "enc", None, None, None),
        P("slide", "enc", None),
        P("slide", None),
        P("slide", "enc", None, None, None),
        P(),
        P(),
        P(),
    )
    out_specs = (
        P("slide", "enc", None, None, None),
        P(("slide", "enc"), None),
        P(("slide", "enc"), None),
    )
    return jax.shard_map(body, mesh=mesh, in_specs=in_specs, out_specs=out_specs, check_vma=False)
```

```python
import functools

import jax
import jax.numpy as jnp
from jax import lax
from jax.experimental import pallas as pl
from jax.experimental.pallas import tpu as pltpu
from jax.sharding import PartitionSpec as P

root_half = 0.7071067811865476
half_log2_e = -0.7213475204444817
log2_inv_root_two_pi = -1.3257480647361592
axes = ("slide", "enc")
hops = (2, 1, 3)
VMEM = pl.BlockSpec(memory_space=pltpu.VMEM)
SMEM = pl.BlockSpec(memory_space=pltpu.SMEM)
HBM = pl.BlockSpec(memory_space=pltpu.HBM)
small_cost = pl.CostEstimate(flops=1000, bytes_accessed=1000, transcendentals=0)
large_cost = pl.CostEstimate(flops=20_000_000_000, bytes_accessed=1000, transcendentals=0)
nt = (((1,), (1,)), ((), ()))
tn = (((0,), (0,)), ((), ()))


def f32_dot(lhs, rhs, dims=(((1,), (0,)), ((), ()))):
    return lax.dot_general(lhs, rhs, dims, preferred_element_type=jnp.float32)


def row_hits(index, size):
    return index == lax.broadcasted_iota(jnp.int32, (index.shape[0], size), 1)


def slot_tables(counts_ref, owners_ref, table_ref, send_ref, place_ref):
    enc, core = lax.axis_index("enc"), lax.axis_index("slide") % 2
    count, y, z = counts_ref[0, enc], enc // 4, enc % 4
    lanes, tiles = counts_ref.shape[1], owners_ref.shape[1]
    slot = lax.broadcasted_iota(jnp.int32, (tiles, tiles), 0)
    other = lax.broadcasted_iota(jnp.int32, (tiles, tiles), 1)
    line = jnp.broadcast_to(owners_ref[...], (tiles, tiles)).astype(jnp.float32)
    owners = jnp.sum(jnp.where(slot == other, line, 0.0), axis=1, keepdims=True)
    same = jnp.where((owners == line) & (other < slot), 1.0, 0.0)
    owners = owners.astype(jnp.int32)
    rank = jnp.sum(same, axis=1, keepdims=True).astype(jnp.int32)
    live = lax.broadcasted_iota(jnp.int32, (tiles, 1), 0) < count
    pick = lambda index, size, on: jnp.where(row_hits(index, size) & on, 1.0, 0.0).astype(jnp.bfloat16)
    hops_y, hops_z = ((owners >> 2) - y) & 3, ((owners & 3) - z) & 3
    table_ref[...] = pick(rank * lanes + owners, table_ref.shape[1], live)
    one, two = (hops_z, hops_y), (hops_y, hops_z)
    near, far = [jnp.where(core == 0, p, q) for p, q in zip(one, two)]
    send_ref[...] = pick(near * 16 + far * 3 + rank, 64, live)
    spots = lax.broadcasted_iota(jnp.int32, (place_ref.shape[0], 1), 0)
    reader = spots & (lanes - 1)
    from_y, from_z = (y - (reader >> 2)) & 3, (z - (reader & 3)) & 3
    near = jnp.where(core == 0, from_z, from_y)
    far = jnp.where(core == 0, from_y, from_z)
    place_ref[...] = pick(far * 16 + near * 3 + (spots >> 4), 64, spots >= 0)


def conv_kernel(counts_ref, owners_ref, x_hbm, k_hbm, up_hbm, down_hbm, *rest):
    normed_ref, mean_ref, table_ref, send_ref, place_ref = rest[0:5]
    weights = rest[5:13]
    xb, kb, xf, kf, cv, sems = rest[13:]
    side = kb.shape[0]
    tiles, width = mean_ref.shape
    cells, reach = side * side, side // 2
    units = weights[0].shape[0]
    sub = units // 4
    slide, enc = lax.axis_index("slide"), lax.axis_index("enc")
    x, core, y = slide // 2, slide % 2, enc // 4
    first = jnp.where(core == 0, x, y)

    def maps_copy(group):
        rows = pl.ds(group * 16, 16)
        return pltpu.make_async_copy(x_hbm.at[:, :, rows, :], xb.at[group], sems.at[group])

    def weight_copy(n):
        goal = lax.rem(first + (hops + (0,))[n % 16 // 4], 4)
        row = jnp.where(core == 0, 8 * goal + n % 4, 8 * (n % 4) + goal) + 4 * core
        start = pl.ds(pl.multiple_of(row * sub, sub), sub)
        source = (up_hbm if n < 16 else down_hbm).at[start, :]
        goal = weights[n // 4].at[pl.ds(n % 4 * sub, sub), :]
        return pltpu.make_async_copy(source, goal, sems.at[3 + n])

    kernel_copy = pltpu.make_async_copy(k_hbm, kb, sems.at[2])
    kernel_copy.start()
    for group in range(tiles // 16):
        maps_copy(group).start()
    slot_tables(counts_ref, owners_ref, table_ref, send_ref, place_ref)
    for n in range(32):
        weight_copy(n).start()
    kernel_copy.wait()
    for n in range(cells):
        kf[n] = jnp.broadcast_to(
            kb[n // side, n % side : n % side + 1].astype(jnp.float32), (8, width)
        )

    @pl.loop(0, tiles // 16)
    def _(group):
        row = pl.multiple_of(group * 16, 16)
        maps_copy(group).wait()
        for n in range(cells):
            xf[n] = xb[group, n // side, n % side].astype(jnp.float32)

        @pl.loop(0, 2 * (width // 128))
        def _(unit):
            lane = pl.multiple_of((unit // 2) * 128, 128)
            half = pl.multiple_of((unit % 2) * 8, 8)
            for i in range(side):
                acc = [None] * side
                for a in range(side):
                    r = i + a - reach
                    if not 0 <= r < side:
                        continue
                    xs = [xf[r * side + j, pl.ds(half, 8), pl.ds(lane, 128)] for j in range(side)]
                    ks = [kf[a * side + b, :, pl.ds(lane, 128)] for b in range(side)]
                    for j in range(side):
                        for b in range(side):
                            c = j + b - reach
                            if 0 <= c < side:
                                term = xs[c] * ks[b]
                                acc[j] = term if acc[j] is None else acc[j] + term
                for j in range(side):
                    cv[i * side + j, pl.ds(half, 8), pl.ds(lane, 128)] = acc[j]

        total = None
        for n in range(cells):
            conv = cv[n]
            centred = conv - jnp.sum(conv, axis=1, keepdims=True) * (1.0 / width)
            var = jnp.sum(centred * centred, axis=1, keepdims=True) * (1.0 / width)
            normed_ref[n, pl.ds(row, 16), :] = (centred * lax.rsqrt(var + 1e-6)).astype(jnp.bfloat16)
            total = xf[n] if total is None else total + xf[n]
        mean_ref[pl.ds(row, 16), :] = total * (1.0 / cells)

    for n in range(32):
        weight_copy(n).wait()


def conv_norm(counts, owners, maps, kernel, up_weight, down_weight, capacity):
    side, _, tiles, width = maps.shape
    cells = side * side
    units = up_weight.shape[0] // 8
    shape = jax.ShapeDtypeStruct
    return pl.pallas_call(
        conv_kernel,
        out_shape=(
            shape((cells, tiles, width), jnp.bfloat16),
            shape((tiles, width), jnp.float32),
            shape((tiles, 16 * capacity), jnp.bfloat16),
            shape((tiles, 64), jnp.bfloat16),
            shape((16 * capacity, 64), jnp.bfloat16),
            *[shape((units, width), jnp.bfloat16)] * 8,
        ),
        in_specs=[SMEM, VMEM] + [HBM] * 4,
        out_specs=(VMEM,) * 13,
        scratch_shapes=[
            pltpu.VMEM((tiles // 16, side, side, 16, width), jnp.bfloat16),
            pltpu.VMEM(kernel.shape, jnp.bfloat16),
            pltpu.VMEM((cells, 16, width), jnp.float32),
            pltpu.VMEM((cells, 8, width), jnp.float32),
            pltpu.VMEM((cells, 16, width), jnp.float32),
            pltpu.SemaphoreType.DMA((35,)),
        ],
        compiler_params=pltpu.CompilerParams(vmem_limit_bytes=46 << 20),
        cost_estimate=small_cost,
        name="conv_norm",
    )(counts, owners.reshape(1, tiles), maps, kernel, up_weight, down_weight)


def gelu_pair(pre):
    cdf = 0.5 + 0.5 * lax.erf(pre * root_half)
    density = jnp.exp2(pre * pre * half_log2_e + log2_inv_root_two_pi)
    return pre * cdf, cdf + pre * density


def block_kernel(*rest):
    parts, sgs = rest[0:2], rest[2:4]
    up_s, dn_s, emb_ref, pay_ref, emb_out, grads = rest[4:]
    units = up_s.shape[0]
    tiles = sgs[0].shape[0]
    scale = 1.0 / (parts[0].shape[0] // tiles)
    up = up_s[...]
    both = jnp.concatenate([sg[...] for sg in sgs for _ in range(128 // tiles)], axis=0)
    dh_both = f32_dot(dn_s[...], both, nt) * scale
    dh = [dh_both[:, 128 * p : 128 * p + 128] for p in range(2)]

    runs, tails = [], []
    for p, ref in enumerate(parts):
        full = ref.shape[0] // 256 * 256
        runs += [(p, at, min(at + 512, full)) for at in range(0, full, 512)]
        for cut in range(full, ref.shape[0], 128):
            tails.append((p, cut, min(128, ref.shape[0] - cut)))
    tails.sort(key=lambda t: -t[2])
    pool = [jnp.zeros((units, 128), jnp.float32) for _ in range(2)]
    column = 0

    def tile(rhs, owners, column):
        pre = f32_dot(up, rhs, nt)
        at = 0
        for who, w in owners:
            hid, slope = gelu_pair(pre[:, at : at + w])
            grads[:, column + at : column + at + w] = (slope * dh[who][:, 0:w]).astype(jnp.bfloat16)
            if w < 128:
                hid = jnp.concatenate([hid, jnp.zeros((units, 128 - w), jnp.float32)], axis=1)
            pool[who] = pool[who] + hid
            at += w

    up_rows, waiting = None, None

    def absorb(todo, up_rows):
        start, size, rhs = todo
        term = f32_dot(grads[:, start : start + size], rhs())
        return term if up_rows is None else up_rows + term

    for p, low, high in runs:
        start = column
        for cut in range(low, high, 256):
            tile(parts[p][cut : cut + 256, :], [(p, 128)] * 2, column)
            column += 256
        if waiting is not None:
            up_rows = absorb(waiting, up_rows)
        waiting = (start, high - low, lambda p=p, low=low, high=high: parts[p][low:high, :])
    start = column
    group, size = [], 0
    for n, (p, cut, w) in enumerate(tails):
        group.append((p, cut, w))
        size += w
        if size == 256 or n == len(tails) - 1:
            rhs = jnp.concatenate([parts[q][c : c + v, :] for q, c, v in group], axis=0)
            tile(rhs, [(q, v) for q, _, v in group], column)
            column += size
            group, size = [], 0
    up_rows = absorb(waiting, up_rows)
    rhs = jnp.concatenate([parts[p][c : c + w, :] for p, c, w in tails], axis=0)
    up_rows = absorb((start, column - start, lambda: rhs), up_rows)
    pick = (
        lax.broadcasted_iota(jnp.int32, (tiles, 128), 0)
        == lax.broadcasted_iota(jnp.int32, (tiles, 128), 1)
    ).astype(jnp.bfloat16)
    flat = []
    for value in pool:
        shift = 64
        while shift >= tiles:
            value = value + pltpu.roll(value, shift, 1)
            shift //= 2
        flat.append(f32_dot(pick, (value * scale).astype(jnp.bfloat16), nt).astype(jnp.bfloat16))
    pay_ref[0:units] = up_rows.astype(jnp.bfloat16)
    emb_out[...] = emb_ref[...] + f32_dot(jnp.concatenate(flat, axis=0), dn_s[...])
    for h in range(2):
        pay_ref[units + h * tiles : units + (h + 1) * tiles] = sgs[h][...]
        pay_ref[units + 2 * tiles : units + 3 * tiles, h * units : (h + 1) * units] = flat[h]


def hidden_block(parts, grads, up, down, emb):
    tiles, width = grads[0].shape
    units = up.shape[0]
    rows = sum(p.shape[0] for p in parts)
    return pl.pallas_call(
        block_kernel,
        out_shape=(
            jax.ShapeDtypeStruct((units + 3 * tiles, width), jnp.bfloat16),
            jax.ShapeDtypeStruct((2 * tiles, width), jnp.float32),
        ),
        in_specs=[VMEM] * 7,
        out_specs=(VMEM, VMEM),
        scratch_shapes=[pltpu.VMEM((units, rows), jnp.bfloat16)],
        compiler_params=pltpu.CompilerParams(vmem_limit_bytes=16 << 20),
        cost_estimate=small_cost,
        name="hidden_block",
    )(*parts, *grads, up, down, emb)


def one_hot_rows(target, rows):
    hit = lax.broadcasted_iota(jnp.int32, (rows, target.shape[1]), 0) == target
    return jnp.where(hit, 1.0, 0.0).astype(jnp.bfloat16)


def regroup(blocks):
    col = lax.broadcasted_iota(jnp.int32, (1, 64), 1)
    spot = col & 15
    far = jnp.where(spot < 3, 0, jnp.where(spot < 6, 1, jnp.where(spot < 9, 2, 3)))
    target = jnp.where(spot < 12, 16 * far + 3 * (col >> 4) + spot - 3 * far, -1)
    return f32_dot(one_hot_rows(target, 64), jnp.concatenate(blocks, axis=0))


def embed_kernel(table_ref, mean_ref, emb_ref, other_ref, *outs):
    tiles = mean_ref.shape[0]
    embed = (mean_ref[...] + emb_ref[0:tiles] + other_ref[...]).astype(jnp.bfloat16)
    rows = f32_dot(table_ref[...], embed, tn).astype(jnp.bfloat16)
    for k, out in enumerate(outs):
        out[...] = rows[16 * k : 16 * k + 16]


def regroup_kernel(*refs):
    rows = regroup([r[...] for r in refs[0:4]]).astype(jnp.bfloat16)
    for k, out in enumerate(refs[4:]):
        out[...] = rows[16 * k : 16 * k + 16]


def small_call(kernel, name, args, width, cost):
    return pl.pallas_call(
        kernel,
        out_shape=(jax.ShapeDtypeStruct((16, width), jnp.bfloat16),) * 4,
        in_specs=[VMEM] * len(args),
        out_specs=(VMEM,) * 4,
        compiler_params=pltpu.CompilerParams(vmem_limit_bytes=4 << 20),
        cost_estimate=cost,
        name=name,
    )(*args)


def embed_rows(table, mean, emb, other):
    args = (table, mean, emb, other)
    return small_call(embed_kernel, "embed_rows", args, mean.shape[1], small_cost)


def regroup_rows(blocks):
    return small_call(regroup_kernel, "regroup_rows", blocks, blocks[0].shape[1], large_cost)


def combine_kernel(a_ref, b_ref, c_ref, d_ref, *outs):
    total = outs[4]
    slide, enc = lax.axis_index("slide"), lax.axis_index("enc")
    x, core, z = slide // 2, slide % 2, enc % 4
    units = total.shape[0]
    width = a_ref.shape[1]
    tiles = (a_ref.shape[0] - units) // 3
    refs = (a_ref, b_ref, c_ref, d_ref)
    up = None
    for r in refs:
        term = r[0:units].astype(jnp.float32)
        up = term if up is None else up + term
    sg = jnp.concatenate([r[units : units + 2 * tiles] for r in refs], axis=0)
    low, high = units + 2 * tiles, units + 3 * tiles
    pool = jnp.concatenate(
        [r[low:high, h * units : (h + 1) * units] for r in refs for h in range(2)], axis=0
    )
    total[:, 0:width] = up
    total[:, width : 2 * width] = f32_dot(pool, sg, tn)
    sub, last = units // 4, units // 16
    for hop in range(4):
        pieces = []
        for i in range(4):
            on_z = i * sub + ((z + hop) & 3) * last
            on_x = ((x + hop) & 3) * sub + i * last
            start = pl.multiple_of(jnp.where(core == 0, on_z, on_x), 8)
            pieces.append(total[pl.ds(start, last), :])
        out = outs[(hop + 3) % 4]
        out[...] = jnp.concatenate(pieces, axis=0).astype(out.dtype)


def combine(payloads, units):
    width = payloads[0].shape[1]
    shape = lambda dtype: jax.ShapeDtypeStruct((units // 4, 2 * width), dtype)
    return pl.pallas_call(
        combine_kernel,
        out_shape=(shape(jnp.bfloat16),) * 3 + (shape(jnp.float32),),
        in_specs=[VMEM] * 4,
        out_specs=(VMEM,) * 4,
        scratch_shapes=[pltpu.VMEM((units, 2 * width), jnp.float32)],
        compiler_params=pltpu.CompilerParams(vmem_limit_bytes=16 << 20),
        cost_estimate=small_cost,
        name="combine",
    )(*payloads)


def second_kernel(own_ref, *rest):
    received, embeds = rest[0:3], rest[3:6]
    own_out, pays, total = rest[6], rest[7:10], rest[10]
    core, enc = lax.axis_index("slide") % 2, lax.axis_index("enc")
    third = jnp.where(core == 0, enc // 4, enc % 4)
    width = own_out.shape[1]
    last = own_ref.shape[0] // 4
    total[...] = own_ref[...] + sum(r[...].astype(jnp.float32) for r in received)
    for hop in range(4):
        rows = pl.ds(pl.multiple_of(((third + hop) & 3) * last, 8), last)
        up, down = total[rows, 0:width], total[rows, width : 2 * width]
        if hop == 0:
            own_out[...] = jnp.concatenate([up, down], axis=0)
        else:
            pays[hop - 1][...] = jnp.concatenate(
                [up, down, embeds[hop - 1][...].astype(jnp.float32)], axis=0
            ).astype(jnp.bfloat16)


def second_sum(own, received, embeds):
    sub, width = own.shape[0], own.shape[1] // 2
    rows = sub // 2
    return pl.pallas_call(
        second_kernel,
        out_shape=(
            jax.ShapeDtypeStruct((rows, width), jnp.float32),
            *[jax.ShapeDtypeStruct((rows + 16, width), jnp.bfloat16)] * 3,
        ),
        in_specs=[VMEM] * 7,
        out_specs=(VMEM,) * 4,
        scratch_shapes=[pltpu.VMEM(own.shape, jnp.float32)],
        compiler_params=pltpu.CompilerParams(vmem_limit_bytes=8 << 20),
        cost_estimate=small_cost,
        name="second_sum",
    )(own, *received, *embeds)


def last_kernel(place_ref, own_ref, embed_ref, a_ref, b_ref, c_ref, up_ref, down_ref, out_ref):
    half = up_ref.shape[0]
    rows = 2 * half
    total = own_ref[...]
    for r in (a_ref, b_ref, c_ref):
        total = total + r[...].astype(jnp.float32)[0:rows]
    up_ref[...] = total[0:half]
    down_ref[...] = total[half:rows]
    embeds = jnp.concatenate(
        [embed_ref[...]] + [r[rows : rows + 16] for r in (a_ref, b_ref, c_ref)], axis=0
    )
    out_ref[...] = f32_dot(place_ref[...], embeds).astype(jnp.bfloat16)


def last_sum(place, own, embed, received):
    rows, width = own.shape
    return pl.pallas_call(
        last_kernel,
        out_shape=(
            jax.ShapeDtypeStruct((rows // 2, width), jnp.float32),
            jax.ShapeDtypeStruct((rows // 2, width), jnp.float32),
            jax.ShapeDtypeStruct((place.shape[0], width), jnp.bfloat16),
        ),
        in_specs=[VMEM] * 6,
        out_specs=(VMEM,) * 3,
        compiler_params=pltpu.CompilerParams(vmem_limit_bytes=4 << 20),
        cost_estimate=small_cost,
        name="last_sum",
    )(place, own, embed, *received)


def move(value, stage, hop):
    spots = {0: (1, 1), 1: (0, 2), 2: (3, 0), 3: (2, 3), 4: (3, 2)}[stage]
    pairs = []
    for x in range(4):
        for core in range(2):
            for y in range(4):
                for z in range(4):
                    here, there = [x, core, y, z], [x, core, y, z]
                    if stage == 0:
                        there[1] = 1 - core
                    else:
                        there[spots[core]] = (there[spots[core]] + hop) % 4
                    line = lambda p: (p[0] * 2 + p[1]) * 16 + p[2] * 4 + p[3]
                    pairs.append((line(here), line(there)))
    return lax.ppermute(value, axes, pairs)


def body(tile_maps, tile_owner, tissue_counts, embed_grad, depth_kernel, up_weight, down_weight):
    lane_count = lax.axis_size("enc")
    maps = jnp.transpose(tile_maps[0], (1, 2, 0, 3))
    side, _, tiles, width = maps.shape
    units = up_weight.shape[0] // 8
    capacity = embed_grad.shape[3]

    fetched = lax.all_to_all(
        jnp.transpose(embed_grad[0, 0], (1, 0, 2)), "enc", split_axis=1, concat_axis=1, tiled=True
    )
    normed, map_mean, table, send_table, place, *weights = conv_norm(
        tissue_counts, tile_owner, maps, depth_kernel, up_weight, down_weight, capacity
    )
    normed = normed.reshape(-1, width)
    sib_normed = move(normed, 0, 0)
    slot_grad = f32_dot(table, fetched.reshape(capacity * lane_count, width)).astype(jnp.bfloat16)
    sib_grad = move(slot_grad, 0, 0)

    emb = jnp.zeros((2 * tiles, width), jnp.float32)
    payloads = []
    for n, hop in enumerate(hops + (0,)):
        if not hop:
            emb, payloads[0] = lax.optimization_barrier((emb, payloads[0]))
        pay, emb = hidden_block(
            (normed, sib_normed), (slot_grad, sib_grad), weights[n], weights[4 + n], emb
        )
        payloads.append(move(pay, 1, hop) if hop else pay)

    other_emb = move(emb[tiles:], 0, 0)
    payloads[1], other_emb = lax.optimization_barrier((payloads[1], other_emb))
    rows_out = embed_rows(send_table, map_mean, emb, other_emb)
    payloads, _ = lax.optimization_barrier((payloads, rows_out))
    *pays, own = combine(payloads, units)
    received = [move(pays[hop - 1], 2, hop) for hop in (1, 2, 3)]
    moved = [move(rows_out[hop], 4, hop) for hop in (1, 2, 3)]
    own_embed, *embeds = regroup_rows((rows_out[0], *moved))
    own, *pays = second_sum(own, received, embeds)
    by_hop = {hop: move(pays[hop - 1], 3, hop) for hop in (1, 2, 3)}
    up_part, down_part, arrived = last_sum(
        place, own, own_embed, [by_hop[hop] for hop in (1, 2, 3)]
    )
    slide_embed = jnp.transpose(arrived.reshape(capacity, lane_count, width), (1, 0, 2))
    return slide_embed[None, None], up_part, down_part


def solution(mesh):
    in_specs = (
        P("slide", "enc", None, None, None),
        P("slide", "enc", None),
        P("slide", None),
        P("slide", "enc", None, None, None),
        P(),
        P(),
        P(),
    )
    out_specs = (
        P("slide", "enc", None, None, None),
        P(("slide", "enc"), None),
        P(("slide", "enc"), None),
    )
    return jax.shard_map(body, mesh=mesh, in_specs=in_specs, out_specs=out_specs, check_vma=False)
```

```python
import functools

import jax
import jax.numpy as jnp
from jax import lax
from jax.experimental import pallas as pl
from jax.experimental.pallas import tpu as pltpu
from jax.sharding import PartitionSpec as P

root_half = 0.7071067811865476
half_log2_e = -0.7213475204444817
log2_inv_root_two_pi = -1.3257480647361592
axes = ("slide", "enc")
hops = (2, 1, 3)
VMEM = pl.BlockSpec(memory_space=pltpu.VMEM)
SMEM = pl.BlockSpec(memory_space=pltpu.SMEM)
HBM = pl.BlockSpec(memory_space=pltpu.HBM)
small_cost = pl.CostEstimate(flops=1000, bytes_accessed=1000, transcendentals=0)
large_cost = pl.CostEstimate(flops=20_000_000_000, bytes_accessed=1000, transcendentals=0)
nt = (((1,), (1,)), ((), ()))
tn = (((0,), (0,)), ((), ()))


def f32_dot(lhs, rhs, dims=(((1,), (0,)), ((), ()))):
    return lax.dot_general(lhs, rhs, dims, preferred_element_type=jnp.float32)


def row_hits(index, size):
    return index == lax.broadcasted_iota(jnp.int32, (index.shape[0], size), 1)


def slot_tables(counts_ref, owners_ref, table_ref, send_ref, place_ref):
    enc, core = lax.axis_index("enc"), lax.axis_index("slide") % 2
    count, y, z = counts_ref[0, enc], enc // 4, enc % 4
    lanes, tiles = counts_ref.shape[1], owners_ref.shape[1]
    slot = lax.broadcasted_iota(jnp.int32, (tiles, tiles), 0)
    other = lax.broadcasted_iota(jnp.int32, (tiles, tiles), 1)
    line = jnp.broadcast_to(owners_ref[...], (tiles, tiles)).astype(jnp.float32)
    owners = jnp.sum(jnp.where(slot == other, line, 0.0), axis=1, keepdims=True)
    same = jnp.where((owners == line) & (other < slot), 1.0, 0.0)
    owners = owners.astype(jnp.int32)
    rank = jnp.sum(same, axis=1, keepdims=True).astype(jnp.int32)
    live = lax.broadcasted_iota(jnp.int32, (tiles, 1), 0) < count
    pick = lambda index, size, on: jnp.where(row_hits(index, size) & on, 1.0, 0.0).astype(jnp.bfloat16)
    hops_y, hops_z = ((owners >> 2) - y) & 3, ((owners & 3) - z) & 3
    table_ref[...] = pick(rank * lanes + owners, table_ref.shape[1], live)
    one, two = (hops_z, hops_y), (hops_y, hops_z)
    near, far = [jnp.where(core == 0, p, q) for p, q in zip(one, two)]
    send_ref[...] = pick(near * 16 + far * 3 + rank, 64, live)
    spots = lax.broadcasted_iota(jnp.int32, (place_ref.shape[0], 1), 0)
    reader = spots & (lanes - 1)
    from_y, from_z = (y - (reader >> 2)) & 3, (z - (reader & 3)) & 3
    near = jnp.where(core == 0, from_z, from_y)
    far = jnp.where(core == 0, from_y, from_z)
    place_ref[...] = pick(far * 16 + near * 3 + (spots >> 4), 64, spots >= 0)


def conv_kernel(counts_ref, owners_ref, x_hbm, k_hbm, up_hbm, down_hbm, *rest):
    normed_ref, mean_ref, table_ref, send_ref, place_ref = rest[0:5]
    weights = rest[5:13]
    xb, kb, xf, kf, cv, sems = rest[13:]
    side = kb.shape[0]
    tiles, width = mean_ref.shape
    cells, reach = side * side, side // 2
    units = weights[0].shape[0]
    sub = units // 4
    slide, enc = lax.axis_index("slide"), lax.axis_index("enc")
    x, core, y = slide // 2, slide % 2, enc // 4
    first = jnp.where(core == 0, x, y)

    def maps_copy(group):
        rows = pl.ds(group * 16, 16)
        return pltpu.make_async_copy(x_hbm.at[:, :, rows, :], xb.at[group], sems.at[group])

    def weight_copy(n):
        goal = lax.rem(first + (hops + (0,))[n % 16 // 4], 4)
        row = jnp.where(core == 0, 8 * goal + n % 4, 8 * (n % 4) + goal) + 4 * core
        start = pl.ds(pl.multiple_of(row * sub, sub), sub)
        source = (up_hbm if n < 16 else down_hbm).at[start, :]
        goal = weights[n // 4].at[pl.ds(n % 4 * sub, sub), :]
        return pltpu.make_async_copy(source, goal, sems.at[3 + n])

    kernel_copy = pltpu.make_async_copy(k_hbm, kb, sems.at[2])
    kernel_copy.start()
    for group in range(tiles // 16):
        maps_copy(group).start()
    slot_tables(counts_ref, owners_ref, table_ref, send_ref, place_ref)
    for n in range(32):
        weight_copy(n).start()
    kernel_copy.wait()
    for n in range(cells):
        kf[n] = jnp.broadcast_to(
            kb[n // side, n % side : n % side + 1].astype(jnp.float32), (8, width)
        )

    @pl.loop(0, tiles // 16)
    def _(group):
        row = pl.multiple_of(group * 16, 16)
        maps_copy(group).wait()
        for n in range(cells):
            xf[n] = xb[group, n // side, n % side].astype(jnp.float32)

        @pl.loop(0, 2 * (width // 128))
        def _(unit):
            lane = pl.multiple_of((unit // 2) * 128, 128)
            half = pl.multiple_of((unit % 2) * 8, 8)
            for i in range(side):
                acc = [None] * side
                for a in range(side):
                    r = i + a - reach
                    if not 0 <= r < side:
                        continue
                    xs = [xf[r * side + j, pl.ds(half, 8), pl.ds(lane, 128)] for j in range(side)]
                    ks = [kf[a * side + b, :, pl.ds(lane, 128)] for b in range(side)]
                    for j in range(side):
                        for b in range(side):
                            c = j + b - reach
                            if 0 <= c < side:
                                term = xs[c] * ks[b]
                                acc[j] = term if acc[j] is None else acc[j] + term
                for j in range(side):
                    cv[i * side + j, pl.ds(half, 8), pl.ds(lane, 128)] = acc[j]

        total = None
        for n in range(cells):
            conv = cv[n]
            centred = conv - jnp.sum(conv, axis=1, keepdims=True) * (1.0 / width)
            var = jnp.sum(centred * centred, axis=1, keepdims=True) * (1.0 / width)
            normed_ref[n, pl.ds(row, 16), :] = (centred * lax.rsqrt(var + 1e-6)).astype(jnp.bfloat16)
            total = xf[n] if total is None else total + xf[n]
        mean_ref[pl.ds(row, 16), :] = total * (1.0 / cells)

    for n in range(32):
        weight_copy(n).wait()


def conv_norm(counts, owners, maps, kernel, up_weight, down_weight, capacity):
    side, _, tiles, width = maps.shape
    cells = side * side
    units = up_weight.shape[0] // 8
    shape = jax.ShapeDtypeStruct
    return pl.pallas_call(
        conv_kernel,
        out_shape=(
            shape((cells, tiles, width), jnp.bfloat16),
            shape((tiles, width), jnp.float32),
            shape((tiles, 16 * capacity), jnp.bfloat16),
            shape((tiles, 64), jnp.bfloat16),
            shape((16 * capacity, 64), jnp.bfloat16),
            *[shape((units, width), jnp.bfloat16)] * 8,
        ),
        in_specs=[SMEM, VMEM] + [HBM] * 4,
        out_specs=(VMEM,) * 13,
        scratch_shapes=[
            pltpu.VMEM((tiles // 16, side, side, 16, width), jnp.bfloat16),
            pltpu.VMEM(kernel.shape, jnp.bfloat16),
            pltpu.VMEM((cells, 16, width), jnp.float32),
            pltpu.VMEM((cells, 8, width), jnp.float32),
            pltpu.VMEM((cells, 16, width), jnp.float32),
            pltpu.SemaphoreType.DMA((35,)),
        ],
        compiler_params=pltpu.CompilerParams(vmem_limit_bytes=46 << 20),
        cost_estimate=small_cost,
        name="conv_norm",
    )(counts, owners.reshape(1, tiles), maps, kernel, up_weight, down_weight)


def gelu_pair(pre):
    cdf = 0.5 + 0.5 * lax.erf(pre * root_half)
    density = jnp.exp2(pre * pre * half_log2_e + log2_inv_root_two_pi)
    return pre * cdf, cdf + pre * density


def block_kernel(*rest):
    parts, sgs = rest[0:2], rest[2:4]
    up_s, dn_s, emb_ref, pay_ref, emb_out, grads = rest[4:]
    units = up_s.shape[0]
    tiles = sgs[0].shape[0]
    scale = 1.0 / (parts[0].shape[0] // tiles)
    up = up_s[...]
    both = jnp.concatenate([sg[...] for sg in sgs for _ in range(128 // tiles)], axis=0)
    dh_both = f32_dot(dn_s[...], both, nt) * scale
    dh = [dh_both[:, 128 * p : 128 * p + 128] for p in range(2)]

    runs, tails = [], []
    for p, ref in enumerate(parts):
        full = ref.shape[0] // 256 * 256
        runs += [(p, at, min(at + 512, full)) for at in range(0, full, 512)]
        for cut in range(full, ref.shape[0], 128):
            tails.append((p, cut, min(128, ref.shape[0] - cut)))
    tails.sort(key=lambda t: -t[2])
    pool = [jnp.zeros((units, 128), jnp.float32) for _ in range(2)]
    column = 0

    def tile(rhs, owners, column):
        pre = f32_dot(up, rhs, nt)
        at = 0
        for who, w in owners:
            hid, slope = gelu_pair(pre[:, at : at + w])
            grads[:, column + at : column + at + w] = (slope * dh[who][:, 0:w]).astype(jnp.bfloat16)
            if w < 128:
                hid = jnp.concatenate([hid, jnp.zeros((units, 128 - w), jnp.float32)], axis=1)
            pool[who] = pool[who] + hid
            at += w

    up_rows, waiting = None, None

    def absorb(todo, up_rows):
        start, size, rhs = todo
        term = f32_dot(grads[:, start : start + size], rhs())
        return term if up_rows is None else up_rows + term

    for p, low, high in runs:
        start = column
        for cut in range(low, high, 256):
            tile(parts[p][cut : cut + 256, :], [(p, 128)] * 2, column)
            column += 256
        if waiting is not None:
            up_rows = absorb(waiting, up_rows)
        waiting = (start, high - low, lambda p=p, low=low, high=high: parts[p][low:high, :])
    start = column
    group, size = [], 0
    for n, (p, cut, w) in enumerate(tails):
        group.append((p, cut, w))
        size += w
        if size == 256 or n == len(tails) - 1:
            rhs = jnp.concatenate([parts[q][c : c + v, :] for q, c, v in group], axis=0)
            tile(rhs, [(q, v) for q, _, v in group], column)
            column += size
            group, size = [], 0
    up_rows = absorb(waiting, up_rows)
    rhs = jnp.concatenate([parts[p][c : c + w, :] for p, c, w in tails], axis=0)
    up_rows = absorb((start, column - start, lambda: rhs), up_rows)
    pick = (
        lax.broadcasted_iota(jnp.int32, (tiles, 128), 0)
        == lax.broadcasted_iota(jnp.int32, (tiles, 128), 1)
    ).astype(jnp.bfloat16)
    flat = []
    for value in pool:
        shift = 64
        while shift >= tiles:
            value = value + pltpu.roll(value, shift, 1)
            shift //= 2
        flat.append(f32_dot(pick, (value * scale).astype(jnp.bfloat16), nt).astype(jnp.bfloat16))
    pay_ref[0:units] = up_rows.astype(jnp.bfloat16)
    emb_out[...] = emb_ref[...] + f32_dot(jnp.concatenate(flat, axis=0), dn_s[...])
    for h in range(2):
        pay_ref[units + h * tiles : units + (h + 1) * tiles] = sgs[h][...]
        pay_ref[units + 2 * tiles : units + 3 * tiles, h * units : (h + 1) * units] = flat[h]


def hidden_block(parts, grads, up, down, emb):
    tiles, width = grads[0].shape
    units = up.shape[0]
    rows = sum(p.shape[0] for p in parts)
    return pl.pallas_call(
        block_kernel,
        out_shape=(
            jax.ShapeDtypeStruct((units + 3 * tiles, width), jnp.bfloat16),
            jax.ShapeDtypeStruct((2 * tiles, width), jnp.float32),
        ),
        in_specs=[VMEM] * 7,
        out_specs=(VMEM, VMEM),
        scratch_shapes=[pltpu.VMEM((units, rows), jnp.bfloat16)],
        compiler_params=pltpu.CompilerParams(vmem_limit_bytes=16 << 20),
        cost_estimate=small_cost,
        name="hidden_block",
    )(*parts, *grads, up, down, emb)


def one_hot_rows(target, rows):
    hit = lax.broadcasted_iota(jnp.int32, (rows, target.shape[1]), 0) == target
    return jnp.where(hit, 1.0, 0.0).astype(jnp.bfloat16)


def regroup(blocks):
    col = lax.broadcasted_iota(jnp.int32, (1, 64), 1)
    spot = col & 15
    far = jnp.where(spot < 3, 0, jnp.where(spot < 6, 1, jnp.where(spot < 9, 2, 3)))
    target = jnp.where(spot < 12, 16 * far + 3 * (col >> 4) + spot - 3 * far, -1)
    return f32_dot(one_hot_rows(target, 64), jnp.concatenate(blocks, axis=0))


def embed_kernel(table_ref, mean_ref, emb_ref, other_ref, *outs):
    tiles = mean_ref.shape[0]
    embed = (mean_ref[...] + emb_ref[0:tiles] + other_ref[...]).astype(jnp.bfloat16)
    rows = f32_dot(table_ref[...], embed, tn).astype(jnp.bfloat16)
    for k, out in enumerate(outs):
        out[...] = rows[16 * k : 16 * k + 16]


def regroup_kernel(*refs):
    rows = regroup([r[...] for r in refs[0:4]]).astype(jnp.bfloat16)
    for k, out in enumerate(refs[4:]):
        out[...] = rows[16 * k : 16 * k + 16]


def small_call(kernel, name, args, width, cost):
    return pl.pallas_call(
        kernel,
        out_shape=(jax.ShapeDtypeStruct((16, width), jnp.bfloat16),) * 4,
        in_specs=[VMEM] * len(args),
        out_specs=(VMEM,) * 4,
        compiler_params=pltpu.CompilerParams(vmem_limit_bytes=4 << 20),
        cost_estimate=cost,
        name=name,
    )(*args)


def embed_rows(table, mean, emb, other):
    args = (table, mean, emb, other)
    return small_call(embed_kernel, "embed_rows", args, mean.shape[1], small_cost)


def regroup_rows(blocks):
    return small_call(regroup_kernel, "regroup_rows", blocks, blocks[0].shape[1], large_cost)


def combine_kernel(a_ref, b_ref, c_ref, d_ref, *outs):
    total = outs[4]
    slide, enc = lax.axis_index("slide"), lax.axis_index("enc")
    x, core, z = slide // 2, slide % 2, enc % 4
    units = total.shape[0]
    width = a_ref.shape[1]
    tiles = (a_ref.shape[0] - units) // 3
    refs = (a_ref, b_ref, c_ref, d_ref)
    up = None
    for r in refs:
        term = r[0:units].astype(jnp.float32)
        up = term if up is None else up + term
    sg = jnp.concatenate([r[units : units + 2 * tiles] for r in refs], axis=0)
    low, high = units + 2 * tiles, units + 3 * tiles
    pool = jnp.concatenate(
        [r[low:high, h * units : (h + 1) * units] for r in refs for h in range(2)], axis=0
    )
    total[:, 0:width] = up
    total[:, width : 2 * width] = f32_dot(pool, sg, tn)
    sub, last = units // 4, units // 16
    for hop in range(4):
        pieces = []
        for i in range(4):
            on_z = i * sub + ((z + hop) & 3) * last
            on_x = ((x + hop) & 3) * sub + i * last
            start = pl.multiple_of(jnp.where(core == 0, on_z, on_x), 8)
            pieces.append(total[pl.ds(start, last), :])
        out = outs[(hop + 3) % 4]
        out[...] = jnp.concatenate(pieces, axis=0).astype(out.dtype)


def combine(payloads, units):
    width = payloads[0].shape[1]
    shape = lambda dtype: jax.ShapeDtypeStruct((units // 4, 2 * width), dtype)
    return pl.pallas_call(
        combine_kernel,
        out_shape=(shape(jnp.bfloat16),) * 3 + (shape(jnp.float32),),
        in_specs=[VMEM] * 4,
        out_specs=(VMEM,) * 4,
        scratch_shapes=[pltpu.VMEM((units, 2 * width), jnp.float32)],
        compiler_params=pltpu.CompilerParams(vmem_limit_bytes=16 << 20),
        cost_estimate=small_cost,
        name="combine",
    )(*payloads)


def second_kernel(own_ref, *rest):
    received, embeds = rest[0:3], rest[3:6]
    own_out, pays, total = rest[6], rest[7:10], rest[10]
    core, enc = lax.axis_index("slide") % 2, lax.axis_index("enc")
    third = jnp.where(core == 0, enc // 4, enc % 4)
    width = own_out.shape[1]
    last = own_ref.shape[0] // 4
    total[...] = own_ref[...] + sum(r[...].astype(jnp.float32) for r in received)
    for hop in range(4):
        rows = pl.ds(pl.multiple_of(((third + hop) & 3) * last, 8), last)
        up, down = total[rows, 0:width], total[rows, width : 2 * width]
        if hop == 0:
            own_out[...] = jnp.concatenate([up, down], axis=0)
        else:
            pays[hop - 1][...] = jnp.concatenate(
                [up, down, embeds[hop - 1][...].astype(jnp.float32)], axis=0
            ).astype(jnp.bfloat16)


def second_sum(own, received, embeds):
    sub, width = own.shape[0], own.shape[1] // 2
    rows = sub // 2
    return pl.pallas_call(
        second_kernel,
        out_shape=(
            jax.ShapeDtypeStruct((rows, width), jnp.float32),
            *[jax.ShapeDtypeStruct((rows + 16, width), jnp.bfloat16)] * 3,
        ),
        in_specs=[VMEM] * 7,
        out_specs=(VMEM,) * 4,
        scratch_shapes=[pltpu.VMEM(own.shape, jnp.float32)],
        compiler_params=pltpu.CompilerParams(vmem_limit_bytes=8 << 20),
        cost_estimate=small_cost,
        name="second_sum",
    )(own, *received, *embeds)


def last_kernel(place_ref, own_ref, embed_ref, a_ref, b_ref, c_ref, up_ref, down_ref, out_ref):
    half = up_ref.shape[0]
    rows = 2 * half
    total = own_ref[...]
    for r in (a_ref, b_ref, c_ref):
        total = total + r[...].astype(jnp.float32)[0:rows]
    up_ref[...] = total[0:half]
    down_ref[...] = total[half:rows]
    embeds = jnp.concatenate(
        [embed_ref[...]] + [r[rows : rows + 16] for r in (a_ref, b_ref, c_ref)], axis=0
    )
    out_ref[...] = f32_dot(place_ref[...], embeds).astype(jnp.bfloat16)


def last_sum(place, own, embed, received):
    rows, width = own.shape
    return pl.pallas_call(
        last_kernel,
        out_shape=(
            jax.ShapeDtypeStruct((rows // 2, width), jnp.float32),
            jax.ShapeDtypeStruct((rows // 2, width), jnp.float32),
            jax.ShapeDtypeStruct((place.shape[0], width), jnp.bfloat16),
        ),
        in_specs=[VMEM] * 6,
        out_specs=(VMEM,) * 3,
        compiler_params=pltpu.CompilerParams(vmem_limit_bytes=4 << 20),
        cost_estimate=small_cost,
        name="last_sum",
    )(place, own, embed, *received)


def move(value, stage, hop):
    spots = {0: (1, 1), 1: (0, 2), 2: (3, 0), 3: (2, 3), 4: (3, 2)}[stage]
    pairs = []
    for x in range(4):
        for core in range(2):
            for y in range(4):
                for z in range(4):
                    here, there = [x, core, y, z], [x, core, y, z]
                    if stage == 0:
                        there[1] = 1 - core
                    else:
                        there[spots[core]] = (there[spots[core]] + hop) % 4
                    line = lambda p: (p[0] * 2 + p[1]) * 16 + p[2] * 4 + p[3]
                    pairs.append((line(here), line(there)))
    return lax.ppermute(value, axes, pairs)


def body(tile_maps, tile_owner, tissue_counts, embed_grad, depth_kernel, up_weight, down_weight):
    lane_count = lax.axis_size("enc")
    maps = jnp.transpose(tile_maps[0], (1, 2, 0, 3))
    side, _, tiles, width = maps.shape
    units = up_weight.shape[0] // 8
    capacity = embed_grad.shape[3]

    fetched = lax.all_to_all(
        jnp.transpose(embed_grad[0, 0], (1, 0, 2)), "enc", split_axis=1, concat_axis=1, tiled=True
    )
    normed, map_mean, table, send_table, place, *weights = conv_norm(
        tissue_counts, tile_owner, maps, depth_kernel, up_weight, down_weight, capacity
    )
    normed = normed.reshape(-1, width)
    sib_normed = move(normed, 0, 0)
    slot_grad = f32_dot(table, fetched.reshape(capacity * lane_count, width)).astype(jnp.bfloat16)
    sib_grad = move(slot_grad, 0, 0)

    emb = jnp.zeros((2 * tiles, width), jnp.float32)
    payloads = []
    for n, hop in enumerate(hops + (0,)):
        if not hop:
            emb, payloads[0] = lax.optimization_barrier((emb, payloads[0]))
        pay, emb = hidden_block(
            (normed, sib_normed), (slot_grad, sib_grad), weights[n], weights[4 + n], emb
        )
        payloads.append(move(pay, 1, hop) if hop else pay)

    other_emb = move(emb[tiles:], 0, 0)
    payloads[1], other_emb = lax.optimization_barrier((payloads[1], other_emb))
    rows_out = embed_rows(send_table, map_mean, emb, other_emb)
    payloads, _ = lax.optimization_barrier((payloads, rows_out))
    *pays, own = combine(payloads, units)
    received = [move(pays[hop - 1], 2, hop) for hop in (1, 3, 2)]
    moved = [move(rows_out[hop], 4, hop) for hop in (1, 2, 3)]
    own_embed, *embeds = regroup_rows((rows_out[0], *moved))
    own, *pays = second_sum(own, received, embeds)
    by_hop = {hop: move(pays[hop - 1], 3, hop) for hop in (1, 3, 2)}
    up_part, down_part, arrived = last_sum(
        place, own, own_embed, [by_hop[hop] for hop in (1, 2, 3)]
    )
    slide_embed = jnp.transpose(arrived.reshape(capacity, lane_count, width), (1, 0, 2))
    return slide_embed[None, None], up_part, down_part


def solution(mesh):
    in_specs = (
        P("slide", "enc", None, None, None),
        P("slide", "enc", None),
        P("slide", None),
        P("slide", "enc", None, None, None),
        P(),
        P(),
        P(),
    )
    out_specs = (
        P("slide", "enc", None, None, None),
        P(("slide", "enc"), None),
        P(("slide", "enc"), None),
    )
    return jax.shard_map(body, mesh=mesh, in_specs=in_specs, out_specs=out_specs, check_vma=False)
```
